32 devices in a mesh: rows: 16 (over z, y, core), diag: 2 (over x).
Axes of the slice: x: 2, y: 2, z: 4, core: 2. Of those that a mesh axis runs over, the one named last changes fastest.
Arguments:
- bins: bfloat16 [4096, 32], P('rows'), may hold values from -6 to 6
- conv_weight: bfloat16 [2, 3, 3, 32, 32], replicated, may hold values from -0.375 to 0.375
- head_weight: bfloat16 [32], replicated, may hold values from -1 to 1
- dilation: int32 [2], replicated, may hold values from 1 to 8, as said below
- tile_table: int32 [16, 8], P('rows', 'diag'), may hold values from 0 to 7, each once within a row
- cotangent: bfloat16 [16, 8, 128, 128], P('rows', 'diag'), may hold values from -0.59765625 to 0.59765625
Outputs:
- predicted: bfloat16 [16, 8, 128, 128], P('rows', 'diag')
- grad_bins: float32 [4096, 32], P(('rows', 'diag'))
- grad_conv: float32 [2, 3, 3, 32, 32], replicated
- grad_head: float32 [32], replicated
The draws below stay inside these ranges and needn't reach their ends.
Inputs may be any that keep to these rules, and one draw needn't show every extreme that they name: `dilation`: one of the 2 dilations equals 8.
All inputs are finite; a program needn't handle non-finite values.
Results may differ from the reference program's by a relative error of at most 0.013.
The reference program's roundings to bfloat16 on the way count: a program that leaves them out, or rounds other values in their place, can miss the bound.
Values may be sent and summed in bfloat16 or wider, within the bound.
A program may use at most 128 MiB of HBM per device.

```python
from functools import partial
import jax
import jax.numpy as jnp
from jax import lax

C = 32
TILE = 128
OFFS = 4
LAYERS = 2
DMAX = 8
BIN_DEV = 256
NB = 4096
TILES_GRP = 8
BAND = 384
N_ROWS = 16


def draw_dilation(key, part):
    key = jax.random.fold_in(key, 7)
    first_key, second_key = jax.random.split(key)
    values = jax.random.randint(first_key, (LAYERS,), 1, DMAX + 1, dtype=jnp.int32)
    chosen = jax.random.randint(second_key, (), 0, LAYERS, dtype=jnp.int32)
    layer_ids = jnp.arange(LAYERS, dtype=jnp.int32)
    return jnp.where(layer_ids == chosen, jnp.int32(DMAX), values).astype(jnp.int32)


def shard_levels(key, shape, cuts, least, high):
    gain, own = 1.0, jax.random.fold_in(key, 6)
    for axis_at, blocks in cuts:
        draws = jnp.exp(jax.random.uniform(jax.random.fold_in(own, axis_at), (blocks,), jnp.float32, least / len(cuts), high / len(cuts)))
        gain = gain * jnp.repeat(draws, shape[axis_at] // blocks).reshape([-1 if axis == axis_at else 1 for axis in range(len(shape))])
    return gain


def gaussian(stream_key, shape, width, bound, cuts=(), held_as=jnp.bfloat16):
    values = width * jax.random.normal(stream_key, shape, jnp.float32)
    if cuts:
        values = values * shard_levels(stream_key, shape, cuts, -0.22, 0.18)
    return jnp.clip(values, -bound, bound).astype(held_as)


def setup_inputs(seed: int = 0) -> dict:
    key_list = jax.random.split(jax.random.key(seed), 7)
    bins = gaussian(key_list[0], (NB, C), 1.0, 6.0, ((0, 16),))
    conv_weight = gaussian(key_list[1], (LAYERS, 3, 3, C, C), (9 * C) ** -0.5, 0.375)
    head_weight = gaussian(key_list[2], (C,), C ** -0.5, 1.0)
    dilation = draw_dilation(jax.random.fold_in(key_list[6], 71), 0)
    tile_table = jax.vmap(lambda own: jax.random.permutation(own, TILES_GRP))(jax.random.split(key_list[4], N_ROWS)).reshape((N_ROWS, TILES_GRP)).astype(jnp.int32)
    cotangent = gaussian(key_list[5], (N_ROWS, TILES_GRP, TILE, TILE), 0.1, 0.59765625, ((0, 16), (1, 2)))
    return dict(bins=bins, conv_weight=conv_weight, head_weight=head_weight, dilation=dilation, tile_table=tile_table, cotangent=cotangent)


def dilated(pair_state, kernel, spacing):
    active = jax.nn.relu(pair_state)
    channels = pair_state.shape[0]
    extent = pair_state.shape[1]
    padded = jnp.pad(active, ((0, 0), (DMAX, DMAX), (DMAX, DMAX)))
    columns = []
    for row_tap in range(3):
        for col_tap in range(3):
            row_start = (DMAX + (row_tap - 1) * spacing).astype(jnp.int32)
            col_start = (DMAX + (col_tap - 1) * spacing).astype(jnp.int32)
            shifted = lax.dynamic_slice(padded, (jnp.int32(0), row_start, col_start), (channels, extent, extent))
            columns.append(shifted.reshape(channels, extent * extent).astype(jnp.bfloat16))
    stacked = jnp.concatenate(columns, 0)
    kernel_mat = kernel.reshape(9 * channels, channels).astype(jnp.bfloat16)
    summed = jnp.dot(kernel_mat.T, stacked, preferred_element_type=jnp.float32)
    return summed.reshape(channels, extent, extent)

def tile_forward(left_bins, right_bins, conv_f, head_f, dilation):
    pair_state = 0.5 * (left_bins.T[:, :, None] + right_bins.T[:, None, :])
    for layer_index in range(conv_f.shape[0]):
        pair_state = pair_state + dilated(pair_state, conv_f[layer_index], dilation[layer_index])
    channels = pair_state.shape[0]
    flattened = pair_state.reshape(channels, -1)
    mapped = jnp.dot(head_f[None, :], flattened, precision=lax.Precision.HIGHEST, preferred_element_type=jnp.float32)
    return mapped.reshape(pair_state.shape[1], pair_state.shape[2])

def tile_mask(row_tile, offset, total_bins):
    position = lax.iota(jnp.int32, TILE)
    first_pos = row_tile * TILE + position[:, None]
    second_pos = (row_tile + offset) * TILE + position[None, :]
    distance = second_pos - first_pos
    return (distance >= 0) & (distance <= BAND) & (second_pos < total_bins)

def tile_pass(left_bins, right_bins, conv_f, head_f, dilation, tile_cot, band_mask):
    mapped, pullback = jax.vjp(partial(tile_forward, dilation=dilation), left_bins, right_bins, conv_f, head_f)
    masked_cot = jnp.where(band_mask, tile_cot.astype(jnp.float32), jnp.zeros_like(mapped))
    grad_left, grad_right, grad_kernel, grad_out = pullback(masked_cot)
    return (mapped.astype(jnp.bfloat16), grad_left, grad_right, grad_kernel, grad_out)

def reference(bins, conv_weight, head_weight, dilation, tile_table, cotangent):
    tile_rows = BIN_DEV // TILE
    padded = jnp.concatenate([bins, jnp.zeros((2 * BIN_DEV, C), bins.dtype)], 0)
    conv_f = conv_weight.astype(jnp.float32)
    head_f = head_weight.astype(jnp.float32)
    flat_table = tile_table.reshape(-1)
    flat_cot = cotangent.reshape(-1, TILE, TILE)
    groups = (jnp.arange(N_ROWS * TILES_GRP, dtype=jnp.int32) // TILES_GRP).astype(jnp.int32)

    def advance(running, element):
        grad_all, grad_kernels, grad_heads = running
        group_index, tile_id, tile_cot = element
        row_tile = (group_index * tile_rows + tile_id // OFFS).astype(jnp.int32)
        offset = (tile_id % OFFS).astype(jnp.int32)
        left_start = (row_tile * TILE).astype(jnp.int32)
        right_start = ((row_tile + offset) * TILE).astype(jnp.int32)
        left_bins = lax.dynamic_slice_in_dim(padded, left_start, TILE, 0).astype(jnp.float32)
        right_bins = lax.dynamic_slice_in_dim(padded, right_start, TILE, 0).astype(jnp.float32)
        band_mask = tile_mask(row_tile, offset, NB)
        mapped, grad_left, grad_right, grad_kernel, grad_out = tile_pass(left_bins, right_bins, conv_f, head_f, dilation, tile_cot, band_mask)
        current = lax.dynamic_slice_in_dim(grad_all, left_start, TILE, 0)
        grad_all = lax.dynamic_update_slice_in_dim(grad_all, current + grad_left, left_start, 0)
        current = lax.dynamic_slice_in_dim(grad_all, right_start, TILE, 0)
        grad_all = lax.dynamic_update_slice_in_dim(grad_all, current + grad_right, right_start, 0)
        return ((grad_all, grad_kernels + grad_kernel, grad_heads + grad_out), mapped)
    start_state = (jnp.zeros((NB + 2 * BIN_DEV, C), jnp.float32), jnp.zeros(conv_weight.shape, jnp.float32), jnp.zeros((C,), jnp.float32))
    final_state, mapped_all = lax.scan(advance, start_state, (groups, flat_table, flat_cot))
    grad_all, grad_kernels, grad_heads = final_state
    predicted = mapped_all.reshape(N_ROWS, TILES_GRP, TILE, TILE)
    return (predicted, grad_all[:NB], grad_kernels, grad_heads)
```

```python
from functools import partial

import jax
import jax.numpy as jnp
from jax import lax
from jax.experimental import pallas as pl
from jax.experimental.pallas import tpu as pltpu
from jax.sharding import PartitionSpec as P

TILE = 128
OFFS = 4
DMAX = 8
BAND = 384
GROUP = 8


def shifted_2(block, axis, distance):
    devices = range(lax.axis_size(axis))
    route = [(i - distance, i) for i in devices if i - distance in devices]
    return lax.ppermute(block, axis, route)


def shifts(value, spacing, lane):
    before = jnp.where(lane >= spacing, pltpu.roll(value, spacing, 1), 0.0)
    after = jnp.where(lane < TILE - spacing, pltpu.roll(value, TILE - spacing, 1), 0.0)
    return before, value, after


def tower_kernel(
    tiles_ref, dil_ref, base_ref,
    left_ref, right_ref, cot_ref, k0_ref, k1_ref, k0t_ref, w1_ref, head_ref,
    pred_ref, gwin_ref, gk0_ref, u1_ref, gh_ref,
    a0_ref, a1_ref, gs_ref, cs_ref, pair_ref, cot_f, cot_b, cot_a, pred_f,
    *, total_bins,
):
    step = pl.program_id(0)
    channels = head_ref.shape[0]
    tile_id = tiles_ref[step]
    d0 = dil_ref[0]
    d1 = dil_ref[1]
    local_row = tile_id // OFFS
    offset = tile_id % OFFS

    @pl.when(step == 0)
    def _():
        for ref in (a0_ref, a1_ref, gs_ref, cs_ref):
            edge = jnp.zeros((DMAX,) + ref.shape[1:], ref.dtype)
            ref[:DMAX] = edge
            ref[TILE + DMAX:] = edge
        for ref in (gwin_ref, gk0_ref, u1_ref, gh_ref):
            ref[...] = jnp.zeros_like(ref)

    lane = lax.broadcasted_iota(jnp.int32, (channels, TILE), 1)
    lane_t = lax.broadcasted_iota(jnp.int32, (TILE, TILE), 1)
    sub_t = lax.broadcasted_iota(jnp.int32, (TILE, TILE), 0)
    sub_c = lax.broadcasted_iota(jnp.int32, (16, TILE), 0)
    distance = offset * TILE + lane_t - sub_t
    second = (base_ref[0] + local_row + offset) * TILE + lane_t
    keep = (distance >= 0) & (distance <= BAND) & (second < total_bins)
    masked = jnp.where(keep, cot_ref[0].astype(jnp.float32), 0.0)
    before, _, after = shifts(masked, d1, lane_t)
    cot_f[...] = masked
    cot_b[...] = before
    cot_a[...] = after
    right = right_ref[0]

    def put(ref, p, value, spacing):
        parts = [part.astype(jnp.bfloat16) for part in shifts(value, spacing, lane)]
        ref[p + DMAX] = jnp.concatenate(parts, 0)

    def near(ref, p, spacing):
        at = p + DMAX
        def column(row):
            return jnp.concatenate([ref[row - spacing], ref[row], ref[row + spacing]], 0)
        return jnp.concatenate([column(at), column(at + 1)], 1)

    def pair0(column, j):
        return 0.5 * (jnp.broadcast_to(column[:, j:j + 1], (channels, TILE)) + right)

    def first(g, _):
        column = left_ref[0, g]
        base = g * GROUP
        for j in range(GROUP):
            p = base + j
            put(a0_ref, p, jnp.maximum(pair0(column, j), 0.0), d0)
            row = jnp.where(
                sub_c == 0, cot_b[pl.ds(p, 1), :],
                jnp.where(sub_c == 1, cot_f[pl.ds(p, 1), :],
                          jnp.where(sub_c == 2, cot_a[pl.ds(p, 1), :], 0.0)))
            cs_ref[p + DMAX] = row.astype(jnp.bfloat16)
        return 0

    lax.fori_loop(0, TILE // GROUP, first, 0)

    def second_layer(g, _):
        column = left_ref[0, g]
        base = g * GROUP
        for j in range(0, GROUP, 2):
            p = base + j
            out = jnp.dot(k0_ref[...], near(a0_ref, p, d0), preferred_element_type=jnp.float32)
            for i in range(2):
                value = pair0(column, j + i) + out[:, i * TILE:(i + 1) * TILE]
                pair_ref[p + i] = value
                put(a1_ref, p + i, jnp.maximum(value, 0.0), d1)
        return 0

    lax.fori_loop(0, TILE // GROUP, second_layer, 0)

    head = head_ref[...]

    def turn(g, carry):
        acc_u, acc_h = carry
        base = g * GROUP
        rows = []
        for j in range(0, GROUP, 2):
            p = base + j
            out = jnp.dot(k1_ref[...], near(a1_ref, p, d1), preferred_element_type=jnp.float32)
            around = near(cs_ref, p, d1)
            back = jnp.dot(w1_ref[...], around, preferred_element_type=jnp.float32)
            at = p + DMAX
            stack = jnp.concatenate([a1_ref[at], a1_ref[at + 1]], 1)
            acc_u = acc_u + lax.dot_general(
                stack, around, (((1,), (1,)), ((), ())), preferred_element_type=jnp.float32)
            for i in range(2):
                value = pair_ref[p + i]
                cot = cot_f[pl.ds(p + i, 1), :]
                pair2 = value + out[:, i * TILE:(i + 1) * TILE]
                rows.append(jnp.sum(head * pair2, 0, keepdims=True))
                acc_h = acc_h + pair2 * cot
                grad = head * cot + jnp.where(value > 0.0, back[:, i * TILE:(i + 1) * TILE], 0.0)
                pair_ref[p + i] = grad
                put(gs_ref, p + i, grad, d0)
        pred_f[pl.ds(pl.multiple_of(base, GROUP), GROUP), :] = jnp.concatenate(rows, 0)
        return acc_u, acc_h

    acc_u, acc_h = lax.fori_loop(
        0, TILE // GROUP, turn, (jnp.zeros(u1_ref.shape, jnp.float32), jnp.zeros(gh_ref.shape, jnp.float32)))
    u1_ref[...] += acc_u
    gh_ref[...] += acc_h
    pred_ref[0] = pred_f[...].astype(jnp.bfloat16)

    def last(g, carry):
        grad_left, grad_right = carry
        column = left_ref[0, g]
        base = g * GROUP
        acc_k = jnp.zeros(gk0_ref.shape, jnp.float32)
        for j in range(0, GROUP, 2):
            p = base + j
            out = jnp.dot(k0t_ref[...], near(gs_ref, p, d0), preferred_element_type=jnp.float32)
            at = p + DMAX
            mid = slice(channels, 2 * channels)
            def center(row):
                return jnp.concatenate(
                    [gs_ref[row - d0, mid], gs_ref[row, mid], gs_ref[row + d0, mid]], 0)
            stack = jnp.concatenate([a0_ref[at], a0_ref[at + 1]], 1)
            around = jnp.concatenate([center(at), center(at + 1)], 1)
            acc_k = acc_k + lax.dot_general(
                stack, around, (((1,), (1,)), ((), ())), preferred_element_type=jnp.float32)
            for i in range(2):
                grad = pair_ref[p + i] + jnp.where(
                    pair0(column, j + i) > 0.0, out[:, i * TILE:(i + 1) * TILE], 0.0)
                grad_right = grad_right + grad
                grad_left = jnp.where(lane == p + i, jnp.sum(grad, 1, keepdims=True), grad_left)
        gk0_ref[...] += acc_k
        return grad_left, grad_right

    zeros = jnp.zeros((channels, TILE), jnp.float32)
    grad_left, grad_right = lax.fori_loop(0, TILE // GROUP, last, (zeros, zeros))
    gwin_ref[local_row] += 0.5 * grad_left
    gwin_ref[local_row + offset] += 0.5 * grad_right


def tower(tiles, dilation, base_row, window, conv_weight, head_weight, cotangent, total_bins, tile_rows):
    slots = tiles.shape[0]
    channels = window.shape[1]
    blocks = window.shape[0] // TILE
    bf16 = jnp.bfloat16
    f32 = jnp.float32
    window = window.astype(f32)
    left = window[:tile_rows * TILE].reshape(tile_rows, TILE // GROUP, GROUP, channels).transpose(0, 1, 3, 2)
    right = window.reshape(blocks, TILE, channels).transpose(0, 2, 1)
    taps = 9 * channels
    k0 = conv_weight[0].reshape(taps, channels).T
    k1 = conv_weight[1].reshape(taps, channels).T
    k0t = conv_weight[0, ::-1, ::-1].transpose(2, 0, 1, 3).reshape(channels, taps)
    head_f = head_weight.astype(f32)
    folded = jnp.sum(conv_weight[1].astype(f32) * head_f, -1)[::-1, ::-1]
    w1 = jnp.pad(folded, ((0, 0), (0, 13), (0, 0))).transpose(2, 0, 1).reshape(channels, 48).astype(bf16)
    head_b = jnp.broadcast_to(head_f[:, None], (channels, TILE))

    def whole(shape):
        return pl.BlockSpec(shape, lambda s, *_: (0,) * len(shape))

    padded = TILE + 2 * DMAX
    outs = pl.pallas_call(
        partial(tower_kernel, total_bins=total_bins),
        grid_spec=pltpu.PrefetchScalarGridSpec(
            num_scalar_prefetch=3,
            grid=(slots,),
            in_specs=[
                pl.BlockSpec((1, TILE // GROUP, channels, GROUP), lambda s, t, d, b: (t[s] // OFFS, 0, 0, 0)),
                pl.BlockSpec((1, channels, TILE), lambda s, t, d, b: (t[s] // OFFS + t[s] % OFFS, 0, 0)),
                pl.BlockSpec((1, TILE, TILE), lambda s, t, d, b: (s, 0, 0)),
                whole(k0.shape), whole(k1.shape), whole(k0t.shape), whole(w1.shape), whole(head_b.shape),
            ],
            out_specs=[
                pl.BlockSpec((1, TILE, TILE), lambda s, t, d, b: (s, 0, 0)),
                whole((blocks, channels, TILE)),
                whole((3 * channels, 3 * channels)),
                whole((3 * channels, 48)),
                whole((channels, TILE)),
            ],
            scratch_shapes=[
                pltpu.VMEM((padded, 3 * channels, TILE), bf16),
                pltpu.VMEM((padded, 3 * channels, TILE), bf16),
                pltpu.VMEM((padded, 3 * channels, TILE), bf16),
                pltpu.VMEM((padded, 16, TILE), bf16),
                pltpu.VMEM((TILE, channels, TILE), f32),
                pltpu.VMEM((TILE, TILE), f32),
                pltpu.VMEM((TILE, TILE), f32),
                pltpu.VMEM((TILE, TILE), f32),
                pltpu.VMEM((TILE, TILE), f32),
            ],
        ),
        out_shape=[
            jax.ShapeDtypeStruct((slots, TILE, TILE), bf16),
            jax.ShapeDtypeStruct((blocks, channels, TILE), f32),
            jax.ShapeDtypeStruct((3 * channels, 3 * channels), f32),
            jax.ShapeDtypeStruct((3 * channels, 48), f32),
            jax.ShapeDtypeStruct((channels, TILE), f32),
        ],
        compiler_params=pltpu.CompilerParams(
            dimension_semantics=("arbitrary",), vmem_limit_bytes=40 * 1024 * 1024),
        name="tower",
    )(tiles, dilation, base_row, left, right, cotangent, k0, k1, k0t, w1, head_b)
    return outs


def on_device(bins, conv_weight, head_weight, dilation, tile_table, cotangent):
    bin_dev = bins.shape[0]
    channels = bins.shape[1]
    tile_rows = bin_dev // TILE
    total_bins = lax.axis_size("rows") * bin_dev
    following = shifted_2(bins, "rows", -1)
    farther = shifted_2(bins[:TILE], "rows", -2)
    window = jnp.concatenate([bins, following, farther], 0)
    base_row = (lax.axis_index("rows") * tile_rows).astype(jnp.int32).reshape(1)
    predicted, gwin, gk0, u1, gh = tower(
        tile_table[0], dilation, base_row, window, conv_weight, head_weight, cotangent[0],
        total_bins, tile_rows)
    near_back = shifted_2(gwin[tile_rows:2 * tile_rows].astype(jnp.bfloat16), "rows", 1).astype(jnp.float32)
    far_back = shifted_2(gwin[2 * tile_rows:].astype(jnp.bfloat16), "rows", 2).astype(jnp.float32)
    own = gwin[:tile_rows] + near_back
    own = own + jnp.pad(far_back, ((0, tile_rows - 1), (0, 0), (0, 0)))
    own = own.transpose(0, 2, 1).reshape(bin_dev, channels)
    grad_bins = lax.psum_scatter(own, "diag", scatter_dimension=0, tiled=True)

    head_sum = jnp.sum(gh, 1)
    u_part = u1.reshape(3, channels, 3, 16)[:, :, :, 1].reshape(-1)
    flat = jnp.concatenate([gk0.reshape(-1), u_part, head_sum])
    flat = lax.psum(flat, ("rows", "diag"))
    cut = 9 * channels * channels
    grad_k0 = flat[:cut].reshape(3, channels, 3, channels)[:, :, ::-1].transpose(2, 0, 1, 3)
    u_sum = flat[cut:cut + 9 * channels].reshape(3, channels, 3)[:, :, ::-1].transpose(2, 0, 1)
    grad_k1 = u_sum[..., None] * head_weight.astype(jnp.float32)
    grad_head = flat[cut + 9 * channels:]
    return (predicted[None], grad_bins, jnp.stack([grad_k0, grad_k1]), grad_head)


def solution(mesh):
    in_specs = (P("rows", None), P(), P(), P(), P("rows", "diag"), P("rows", "diag", None, None))
    out_specs = (P("rows", "diag", None, None), P(("rows", "diag"), None), P(), P())
    return jax.shard_map(
        on_device, mesh=mesh, in_specs=in_specs, out_specs=out_specs, check_vma=False
    )
```

```python
from functools import partial

import jax
import jax.numpy as jnp
from jax import lax
from jax.experimental import pallas as pl
from jax.experimental.pallas import tpu as pltpu
from jax.sharding import PartitionSpec as P

TILE = 128
OFFS = 4
DMAX = 8
BAND = 384
GROUP = 8


def shifted_2(block, axis, distance):
    devices = range(lax.axis_size(axis))
    route = [(i - distance, i) for i in devices if i - distance in devices]
    return lax.ppermute(block, axis, route)


def shifts(value, spacing, lane):
    before = jnp.where(lane >= spacing, pltpu.roll(value, spacing, 1), 0.0)
    after = jnp.where(lane < TILE - spacing, pltpu.roll(value, TILE - spacing, 1), 0.0)
    return before, value, after


def tower_kernel(
    tiles_ref, dil_ref, base_ref,
    left_ref, right_ref, cot_ref, k0_ref, k1_ref, k0t_ref, w1_ref, head_ref,
    pred_ref, gwin_ref, gk0_ref, u1_ref, gh_ref,
    a0_ref, a1_ref, gs_ref, cs_ref, y0_ref, y1_ref, pair_ref, cot_f, cot_b, cot_a, pred_f,
    *, total_bins,
):
    step = pl.program_id(0)
    channels = head_ref.shape[0]
    tile_id = tiles_ref[step]
    d0 = dil_ref[0]
    d1 = dil_ref[1]
    local_row = tile_id // OFFS
    offset = tile_id % OFFS

    @pl.when(step == 0)
    def _():
        for ref in (gs_ref, cs_ref, y0_ref, y1_ref):
            edge = jnp.zeros((DMAX,) + ref.shape[1:], ref.dtype)
            ref[:DMAX] = edge
            ref[TILE + DMAX:] = edge
        for ref in (gwin_ref, gk0_ref, u1_ref, gh_ref):
            ref[...] = jnp.zeros_like(ref)

    lane = lax.broadcasted_iota(jnp.int32, (channels, TILE), 1)
    lane_t = lax.broadcasted_iota(jnp.int32, (TILE, TILE), 1)
    sub_t = lax.broadcasted_iota(jnp.int32, (TILE, TILE), 0)
    sub_c = lax.broadcasted_iota(jnp.int32, (16, TILE), 0)
    distance = offset * TILE + lane_t - sub_t
    second = (base_ref[0] + local_row + offset) * TILE + lane_t
    keep = (distance >= 0) & (distance <= BAND) & (second < total_bins)
    masked = jnp.where(keep, cot_ref[0].astype(jnp.float32), 0.0)
    before, _, after = shifts(masked, d1, lane_t)
    cot_f[...] = masked
    cot_b[...] = before
    cot_a[...] = after
    right = right_ref[0]

    def stack(value, spacing):
        return jnp.concatenate([part.astype(jnp.bfloat16) for part in shifts(value, spacing, lane)], 0)

    def spread(ref, p, kernel, pair):
        out = jnp.dot(kernel, jnp.concatenate(pair, 1), preferred_element_type=jnp.float32)
        ref[p + DMAX] = out[:, :TILE]
        ref[p + DMAX + 1] = out[:, TILE:]

    def collect(ref, p, spacing):
        at = p + DMAX
        return (ref[at - spacing, :channels] + ref[at, channels:2 * channels]
                + ref[at + spacing, 2 * channels:])

    def near(ref, p, spacing):
        at = p + DMAX
        def column(row):
            return jnp.concatenate([ref[row - spacing], ref[row], ref[row + spacing]], 0)
        return jnp.concatenate([column(at), column(at + 1)], 1)

    def pair0(column, j):
        return 0.5 * (jnp.broadcast_to(column[:, j:j + 1], (channels, TILE)) + right)

    def first(g, _):
        column = left_ref[0, g]
        base = g * GROUP
        for j in range(0, GROUP, 2):
            pair = []
            for i in range(2):
                p = base + j + i
                pair.append(stack(jnp.maximum(pair0(column, j + i), 0.0), d0))
                a0_ref[p] = pair[i]
                row = jnp.where(
                    sub_c == 0, cot_b[pl.ds(p, 1), :],
                    jnp.where(sub_c == 1, cot_f[pl.ds(p, 1), :],
                              jnp.where(sub_c == 2, cot_a[pl.ds(p, 1), :], 0.0)))
                cs_ref[p + DMAX] = row.astype(jnp.bfloat16)
            spread(y0_ref, base + j, k0_ref[...], pair)
        return 0

    lax.fori_loop(0, TILE // GROUP, first, 0)

    def second_layer(g, _):
        column = left_ref[0, g]
        base = g * GROUP
        for j in range(0, GROUP, 2):
            pair = []
            for i in range(2):
                p = base + j + i
                value = pair0(column, j + i) + collect(y0_ref, p, d0)
                pair_ref[p] = value
                pair.append(stack(jnp.maximum(value, 0.0), d1))
                a1_ref[p] = pair[i]
            spread(y1_ref, base + j, k1_ref[...], pair)
        return 0

    lax.fori_loop(0, TILE // GROUP, second_layer, 0)

    head = head_ref[...]

    def turn(g, carry):
        acc_u, acc_h = carry
        base = g * GROUP
        rows = []
        for j in range(0, GROUP, 2):
            p = base + j
            around = near(cs_ref, p, d1)
            back = jnp.dot(w1_ref[...], around, preferred_element_type=jnp.float32)
            acts = jnp.concatenate([a1_ref[p], a1_ref[p + 1]], 1)
            acc_u = acc_u + lax.dot_general(
                acts, around, (((1,), (1,)), ((), ())), preferred_element_type=jnp.float32)
            pair = []
            for i in range(2):
                value = pair_ref[p + i]
                cot = cot_f[pl.ds(p + i, 1), :]
                pair2 = value + collect(y1_ref, p + i, d1)
                rows.append(jnp.sum(head * pair2, 0, keepdims=True))
                acc_h = acc_h + pair2 * cot
                grad = head * cot + jnp.where(value > 0.0, back[:, i * TILE:(i + 1) * TILE], 0.0)
                pair_ref[p + i] = grad
                pair.append(stack(grad, d0))
                gs_ref[p + i + DMAX] = grad.astype(jnp.bfloat16)
            spread(y0_ref, p, k0t_ref[...], pair)
        pred_f[pl.ds(pl.multiple_of(base, GROUP), GROUP), :] = jnp.concatenate(rows, 0)
        return acc_u, acc_h

    acc_u, acc_h = lax.fori_loop(
        0, TILE // GROUP, turn, (jnp.zeros(u1_ref.shape, jnp.float32), jnp.zeros(gh_ref.shape, jnp.float32)))
    u1_ref[...] += acc_u
    gh_ref[...] += acc_h
    pred_ref[0] = pred_f[...].astype(jnp.bfloat16)

    def last(g, carry):
        grad_left, grad_right = carry
        column = left_ref[0, g]
        base = g * GROUP
        acc_k = jnp.zeros(gk0_ref.shape, jnp.float32)
        for j in range(0, GROUP, 2):
            p = base + j
            acts = jnp.concatenate([a0_ref[p], a0_ref[p + 1]], 1)
            acc_k = acc_k + lax.dot_general(
                acts, near(gs_ref, p, d0), (((1,), (1,)), ((), ())), preferred_element_type=jnp.float32)
            for i in range(2):
                grad = pair_ref[p + i] + jnp.where(
                    pair0(column, j + i) > 0.0, collect(y0_ref, p + i, d0), 0.0)
                grad_right = grad_right + grad
                grad_left = jnp.where(lane == p + i, jnp.sum(grad, 1, keepdims=True), grad_left)
        gk0_ref[...] += acc_k
        return grad_left, grad_right

    zeros = jnp.zeros((channels, TILE), jnp.float32)
    grad_left, grad_right = lax.fori_loop(0, TILE // GROUP, last, (zeros, zeros))
    gwin_ref[local_row] += 0.5 * grad_left
    gwin_ref[local_row + offset] += 0.5 * grad_right


def tower(tiles, dilation, base_row, window, conv_weight, head_weight, cotangent, total_bins, tile_rows):
    slots = tiles.shape[0]
    channels = window.shape[1]
    blocks = window.shape[0] // TILE
    bf16 = jnp.bfloat16
    f32 = jnp.float32
    window = window.astype(f32)
    left = window[:tile_rows * TILE].reshape(tile_rows, TILE // GROUP, GROUP, channels).transpose(0, 1, 3, 2)
    right = window.reshape(blocks, TILE, channels).transpose(0, 2, 1)
    width = 3 * channels
    k0 = conv_weight[0].transpose(0, 3, 1, 2).reshape(width, width)
    k1 = conv_weight[1].transpose(0, 3, 1, 2).reshape(width, width)
    k0t = conv_weight[0, ::-1, ::-1].transpose(0, 2, 1, 3).reshape(width, width)
    head_f = head_weight.astype(f32)
    folded = jnp.sum(conv_weight[1].astype(f32) * head_f, -1)[::-1, ::-1]
    w1 = jnp.pad(folded, ((0, 0), (0, 13), (0, 0))).transpose(2, 0, 1).reshape(channels, 48).astype(bf16)
    head_b = jnp.broadcast_to(head_f[:, None], (channels, TILE))

    def whole(shape):
        return pl.BlockSpec(shape, lambda s, *_: (0,) * len(shape))

    padded = TILE + 2 * DMAX
    outs = pl.pallas_call(
        partial(tower_kernel, total_bins=total_bins),
        grid_spec=pltpu.PrefetchScalarGridSpec(
            num_scalar_prefetch=3,
            grid=(slots,),
            in_specs=[
                pl.BlockSpec((1, TILE // GROUP, channels, GROUP), lambda s, t, d, b: (t[s] // OFFS, 0, 0, 0)),
                pl.BlockSpec((1, channels, TILE), lambda s, t, d, b: (t[s] // OFFS + t[s] % OFFS, 0, 0)),
                pl.BlockSpec((1, TILE, TILE), lambda s, t, d, b: (s, 0, 0)),
                whole(k0.shape), whole(k1.shape), whole(k0t.shape), whole(w1.shape), whole(head_b.shape),
            ],
            out_specs=[
                pl.BlockSpec((1, TILE, TILE), lambda s, t, d, b: (s, 0, 0)),
                whole((blocks, channels, TILE)),
                whole((3 * channels, 3 * channels)),
                whole((3 * channels, 48)),
                whole((channels, TILE)),
            ],
            scratch_shapes=[
                pltpu.VMEM((TILE, width, TILE), bf16),
                pltpu.VMEM((TILE, width, TILE), bf16),
                pltpu.VMEM((padded, channels, TILE), bf16),
                pltpu.VMEM((padded, 16, TILE), bf16),
                pltpu.VMEM((padded, width, TILE), f32),
                pltpu.VMEM((padded, width, TILE), f32),
                pltpu.VMEM((TILE, channels, TILE), f32),
                pltpu.VMEM((TILE, TILE), f32),
                pltpu.VMEM((TILE, TILE), f32),
                pltpu.VMEM((TILE, TILE), f32),
                pltpu.VMEM((TILE, TILE), f32),
            ],
        ),
        out_shape=[
            jax.ShapeDtypeStruct((slots, TILE, TILE), bf16),
            jax.ShapeDtypeStruct((blocks, channels, TILE), f32),
            jax.ShapeDtypeStruct((3 * channels, 3 * channels), f32),
            jax.ShapeDtypeStruct((3 * channels, 48), f32),
            jax.ShapeDtypeStruct((channels, TILE), f32),
        ],
        compiler_params=pltpu.CompilerParams(
            dimension_semantics=("arbitrary",), vmem_limit_bytes=40 * 1024 * 1024),
        name="tower",
    )(tiles, dilation, base_row, left, right, cotangent, k0, k1, k0t, w1, head_b)
    return outs


def steps_of(size):
    steps, low = [], 1
    while low < size:
        span = min(4, size // low)
        steps.append([low * e for e in range(1, span)])
        low *= span
    return steps


def exchange_kernel(
    rows_n, diag_n, tile_rows, per,
    flat_ref, gwin_ref, sum_ref, bins_ref,
    part_ref, got_ref, near_ref, far_ref, own_got, near_got, far_got,
    sum_send, sum_recv, own_send, own_recv, near_send, near_recv, far_send, far_recv,
):
    g = lax.axis_index("rows")
    d = lax.axis_index("diag")
    count = bins_ref.shape[0]
    mesh_id = pl.DeviceIdType.MESH
    steps = [("rows", e) for e in steps_of(rows_n)] + [("diag", e) for e in steps_of(diag_n)]

    def start_of(index):
        return index * per // TILE

    def at(row, diag):
        return {"rows": row, "diag": diag}

    def partner(axis, e):
        return at(g ^ e, d) if axis == "rows" else at(g, d ^ e)

    barrier = pltpu.get_barrier_semaphore()

    def greet(device):
        pl.semaphore_signal(barrier, inc=1, device_id=device, device_id_type=mesh_id)

    met = 0
    for axis, group in steps:
        for e in group:
            greet(partner(axis, e))
            met += 1
    for e in range(1, diag_n):
        greet(at(g, d ^ e))
        met += 1
    firsts = sum(1 for index in range(diag_n) if index * per // TILE == 0)
    for e in range(diag_n):
        @pl.when(g >= 1)
        def _():
            greet(at(g - 1, d ^ e))

        @pl.when((g >= 2) & (start_of(d) == 0))
        def _():
            greet(at(g - 2, d ^ e))
    to_near = 1 - (g + 1) // rows_n
    to_far = 1 - (g + 2) // rows_n
    pl.semaphore_wait(barrier, met + diag_n * to_near + firsts * to_far)

    def remote(src, dst, send, recv, device):
        return pltpu.make_async_remote_copy(
            src_ref=src, dst_ref=dst, send_sem=send, recv_sem=recv,
            device_id=device, device_id_type=mesh_id)

    def sum_copy(step, slot, axis, e):
        src = flat_ref if step == 0 else part_ref.at[step - 1]
        return remote(src, got_ref.at[slot], sum_send.at[slot], sum_recv.at[slot], partner(axis, e))

    def own_copy(e):
        src = gwin_ref.at[pl.ds(start_of(d ^ e), count)]
        return remote(src, own_got.at[e - 1], own_send.at[e - 1], own_recv.at[e - 1], at(g, d ^ e))

    def near_copy(e):
        src = near_ref.at[pl.ds(start_of(d ^ e), count)]
        return remote(src, near_got.at[e], near_send.at[e], near_recv.at[e], at(g + 1, d ^ e))

    def far_copy(e):
        return remote(far_ref, far_got.at[e], far_send.at[e], far_recv.at[e], at(g + 2, d ^ e))

    sends_near = g + 1 < rows_n
    gets_near = g >= 1
    gets_far = (g >= 2) & (start_of(d) == 0)

    def sends_far(e):
        return (g + 2 < rows_n) & (start_of(d ^ e) == 0)

    near_ref[...] = gwin_ref[tile_rows:2 * tile_rows].astype(jnp.bfloat16)
    far_ref[...] = gwin_ref[2 * tile_rows].astype(jnp.bfloat16)
    slot = 0
    value = flat_ref[...]
    copies = []
    for step, (axis, group) in enumerate(steps):
        if step > 0:
            part_ref[step - 1] = value
        here = [sum_copy(step, slot + i, axis, e) for i, e in enumerate(group)]
        for copy in here:
            copy.start()
        if step == 0:
            for e in range(1, diag_n):
                own_copy(e).start()
            for e in range(diag_n):
                pl.when(sends_near)(near_copy(e).start)
                pl.when(sends_far(e))(far_copy(e).start)
        for copy in here:
            copy.wait_recv()
        others = [got_ref[slot + i] for i in range(len(group))]
        value = value + others[0]
        if len(group) == 3:
            value = value + (others[1] + others[2])
        slot += len(group)
        copies += here
    sum_ref[...] = value

    bins_ref[...] = gwin_ref[pl.ds(start_of(d), count)]
    for e in range(1, diag_n):
        own_copy(e).wait_recv()
        bins_ref[...] += own_got[e - 1]

    @pl.when(gets_near)
    def _():
        for e in range(diag_n):
            near_copy(e).wait_recv()
            bins_ref[...] += near_got[e].astype(jnp.float32)

    @pl.when(gets_far)
    def _():
        for e in range(diag_n):
            far_copy(e).wait_recv()
            bins_ref[0] += far_got[e].astype(jnp.float32)

    for copy in copies:
        copy.wait_send()
    for e in range(1, diag_n):
        own_copy(e).wait_send()
    for e in range(diag_n):
        pl.when(sends_near)(near_copy(e).wait_send)
        pl.when(sends_far(e))(far_copy(e).wait_send)


def exchange(flat, gwin, tile_rows):
    rows_n = lax.axis_size("rows")
    diag_n = lax.axis_size("diag")
    per = tile_rows * TILE // diag_n
    count = max(1, per // TILE)
    steps = steps_of(rows_n) + steps_of(diag_n)
    slots = sum(len(group) for group in steps)
    channels = gwin.shape[1]
    block = (channels, TILE)
    f32, bf16 = jnp.float32, jnp.bfloat16
    dma = pltpu.SemaphoreType.DMA
    others = max(1, diag_n - 1)
    vmem = pl.BlockSpec(memory_space=pltpu.VMEM)
    total, bins = pl.pallas_call(
        partial(exchange_kernel, rows_n, diag_n, tile_rows, per),
        out_shape=[jax.ShapeDtypeStruct(flat.shape, f32), jax.ShapeDtypeStruct((count,) + block, f32)],
        in_specs=[vmem] * 2,
        out_specs=[vmem] * 2,
        scratch_shapes=[
            pltpu.VMEM((len(steps),) + flat.shape, f32),
            pltpu.VMEM((slots,) + flat.shape, f32),
            pltpu.VMEM((tile_rows,) + block, bf16),
            pltpu.VMEM(block, bf16),
            pltpu.VMEM((others, count) + block, f32),
            pltpu.VMEM((diag_n, count) + block, bf16),
            pltpu.VMEM((diag_n,) + block, bf16),
            dma((slots,)), dma((slots,)), dma((others,)), dma((others,)),
            dma((diag_n,)), dma((diag_n,)), dma((diag_n,)), dma((diag_n,)),
        ],
        compiler_params=pltpu.CompilerParams(collective_id=0, has_side_effects=True),
        name="exchange",
    )(flat, gwin)
    bins = bins.transpose(0, 2, 1).reshape(count * TILE, channels)
    if per < TILE:
        inside = lax.axis_index("diag") * per % TILE
        bins = lax.dynamic_slice_in_dim(bins, inside, per, 0)
    return total, bins


def on_device(bins, conv_weight, head_weight, dilation, tile_table, cotangent):
    bin_dev = bins.shape[0]
    channels = bins.shape[1]
    tile_rows = bin_dev // TILE
    total_bins = lax.axis_size("rows") * bin_dev
    following = shifted_2(bins, "rows", -1)
    farther = shifted_2(bins[:TILE], "rows", -2)
    window = jnp.concatenate([bins, following, farther], 0)
    base_row = (lax.axis_index("rows") * tile_rows).astype(jnp.int32).reshape(1)
    predicted, gwin, gk0, u1, gh = tower(
        tile_table[0], dilation, base_row, window, conv_weight, head_weight, cotangent[0],
        total_bins, tile_rows)
    width = 3 * channels
    head_sum = jnp.pad(jnp.sum(gh, 1), (0, width - channels))[:, None]
    flat = jnp.concatenate([gk0, u1[:, 1::16], head_sum], 1)
    flat = jnp.pad(flat, ((0, 0), (0, TILE - flat.shape[1])))
    total, grad_bins = exchange(flat, gwin, tile_rows)
    grad_k0 = total[:, :width].reshape(3, channels, 3, channels)[:, :, ::-1].transpose(2, 0, 1, 3)
    u_sum = total[:, width:width + 3].reshape(3, channels, 3)[:, :, ::-1].transpose(2, 0, 1)
    grad_k1 = u_sum[..., None] * head_weight.astype(jnp.float32)
    grad_head = total[:channels, width + 3]
    return (predicted[None], grad_bins, jnp.stack([grad_k0, grad_k1]), grad_head)


def solution(mesh):
    in_specs = (P("rows", None), P(), P(), P(), P("rows", "diag"), P("rows", "diag", None, None))
    out_specs = (P("rows", "diag", None, None), P(("rows", "diag"), None), P(), P())
    return jax.shard_map(
        on_device, mesh=mesh, in_specs=in_specs, out_specs=out_specs, check_vma=False
    )
```

```python
from functools import partial

import jax
import jax.numpy as jnp
from jax import lax
from jax.experimental import pallas as pl
from jax.experimental.pallas import tpu as pltpu
from jax.sharding import PartitionSpec as P

TILE = 128
OFFS = 4
DMAX = 8
BAND = 384
GROUP = 8
OUTSIDE = -1e30


def shifted_2(block, axis, distance):
    devices = range(lax.axis_size(axis))
    route = [(i - distance, i) for i in devices if i - distance in devices]
    return lax.ppermute(block, axis, route)


def shifts(value, spacing, lane):
    before = jnp.where(lane >= spacing, pltpu.roll(value, spacing, 1), 0.0)
    after = jnp.where(lane < TILE - spacing, pltpu.roll(value, TILE - spacing, 1), 0.0)
    return before, value, after


def tower_kernel(
    tiles_ref, dil_ref, base_ref,
    left_ref, right_ref, cot_ref, k0_ref, k1_ref, k0t_ref, head_ref,
    pred_ref, gwin_ref, gk0_ref, u1_ref, gh_ref,
    a0_ref, a1_ref, gs_ref, cs_ref, pair_ref, pair1_ref, right3_ref, cot_f, cot_b, cot_a, pred_f,
    *, total_bins,
):
    step = pl.program_id(0)
    channels = head_ref.shape[0]
    tile_id = tiles_ref[step]
    d0 = dil_ref[0]
    d1 = dil_ref[1]
    local_row = tile_id // OFFS
    offset = tile_id % OFFS

    @pl.when(step == 0)
    def _():
        for ref in (a0_ref, a1_ref, gs_ref, cs_ref):
            edge = jnp.zeros((DMAX,) + ref.shape[1:], ref.dtype)
            ref[:DMAX] = edge
            ref[TILE + DMAX:] = edge
        for ref in (gwin_ref, gk0_ref, u1_ref, gh_ref):
            ref[...] = jnp.zeros_like(ref)

    lane = lax.broadcasted_iota(jnp.int32, (channels, TILE), 1)
    lane_t = lax.broadcasted_iota(jnp.int32, (TILE, TILE), 1)
    sub_t = lax.broadcasted_iota(jnp.int32, (TILE, TILE), 0)
    sub_c = lax.broadcasted_iota(jnp.int32, (16, TILE), 0)
    distance = offset * TILE + lane_t - sub_t
    second = (base_ref[0] + local_row + offset) * TILE + lane_t
    keep = (distance >= 0) & (distance <= BAND) & (second < total_bins)
    masked = jnp.where(keep, cot_ref[0].astype(jnp.float32), 0.0)
    before, _, after = shifts(masked, d1, lane_t)
    cot_f[...] = masked
    cot_b[...] = before
    cot_a[...] = after
    right = right_ref[0]
    right3_ref[:channels] = jnp.where(lane >= d0, pltpu.roll(right, d0, 1), OUTSIDE)
    right3_ref[channels:2 * channels] = right
    right3_ref[2 * channels:] = jnp.where(lane < TILE - d0, pltpu.roll(right, TILE - d0, 1), OUTSIDE)

    def put(ref, p, value, spacing):
        parts = [part.astype(jnp.bfloat16) for part in shifts(value, spacing, lane)]
        ref[p + DMAX] = jnp.concatenate(parts, 0)

    def column(ref, row, spacing):
        return [ref[row - spacing], ref[row], ref[row + spacing]]

    def beside(columns):
        return jnp.concatenate([jnp.concatenate(parts, 0) for parts in columns], 1)

    def transposed_dot(x, y):
        return lax.dot_general(x, y, (((1,), (1,)), ((), ())), preferred_element_type=jnp.float32)

    def first(g, _):
        left = left_ref[0, g]
        for j in range(GROUP):
            p = g * GROUP + j
            one = jnp.broadcast_to(left[:, j:j + 1], (channels, TILE))
            pairs = 0.5 * (jnp.concatenate([one] * 3, 0) + right3_ref[...])
            pair_ref[p] = pairs[channels:2 * channels]
            a0_ref[p + DMAX] = jnp.maximum(pairs, 0.0).astype(jnp.bfloat16)
            row = jnp.where(
                sub_c == 0, cot_b[pl.ds(p, 1), :],
                jnp.where(sub_c == 1, cot_f[pl.ds(p, 1), :],
                          jnp.where(sub_c == 2, cot_a[pl.ds(p, 1), :], 0.0)))
            cs_ref[p + DMAX] = row.astype(jnp.bfloat16)
        return 0

    lax.fori_loop(0, TILE // GROUP, first, 0)

    def second_layer(g, _):
        for j in range(0, GROUP, 2):
            p = g * GROUP + j
            at = p + DMAX
            around = beside([column(a0_ref, at + i, d0) for i in range(2)])
            out = jnp.dot(k0_ref[...], around, preferred_element_type=jnp.float32)
            for i in range(2):
                value = pair_ref[p + i] + out[:, i * TILE:(i + 1) * TILE]
                pair1_ref[p + i] = value
                put(a1_ref, p + i, jnp.maximum(value, 0.0), d1)
        return 0

    lax.fori_loop(0, TILE // GROUP, second_layer, 0)

    head = head_ref[...]

    def turn(g, carry):
        acc_u, acc_h = carry
        base = g * GROUP
        rows = []
        for j in range(0, GROUP, 2):
            p = base + j
            at = p + DMAX
            around = beside([column(a1_ref, at + i, d1) + column(cs_ref, at + i, d1) for i in range(2)])
            out = jnp.dot(k1_ref[...], around, preferred_element_type=jnp.float32)
            for i in range(2):
                value = pair1_ref[p + i]
                cot = cot_f[pl.ds(p + i, 1), :]
                pair2 = value + out[:channels, i * TILE:(i + 1) * TILE]
                rows.append(jnp.sum(head * pair2, 0, keepdims=True))
                acc_h = acc_h + pair2 * cot
                grad = head * cot + jnp.where(value > 0.0, out[channels:, i * TILE:(i + 1) * TILE], 0.0)
                pair_ref[p + i] = grad
                put(gs_ref, p + i, grad, d0)
        pred_f[pl.ds(pl.multiple_of(base, GROUP), GROUP), :] = jnp.concatenate(rows, 0)
        every = [base + DMAX + j for j in range(GROUP)]
        acc_u = acc_u + transposed_dot(
            beside([[a1_ref[at]] for at in every]), beside([column(cs_ref, at, d1) for at in every]))
        return acc_u, acc_h

    acc_u, acc_h = lax.fori_loop(
        0, TILE // GROUP, turn, (jnp.zeros(u1_ref.shape, jnp.float32), jnp.zeros(gh_ref.shape, jnp.float32)))
    u1_ref[...] += acc_u
    gh_ref[...] += acc_h
    pred_ref[0] = pred_f[...].astype(jnp.bfloat16)
    mid = slice(channels, 2 * channels)

    def last(g, carry):
        grad_left, grad_right = carry
        base = g * GROUP
        for j in range(0, GROUP, 2):
            p = base + j
            at = p + DMAX
            around = beside([column(gs_ref, at + i, d0) for i in range(2)])
            out = jnp.dot(k0t_ref[...], around, preferred_element_type=jnp.float32)
            for i in range(2):
                active = a0_ref[at + i, mid].astype(jnp.float32) > 0.0
                grad = pair_ref[p + i] + jnp.where(active, out[:, i * TILE:(i + 1) * TILE], 0.0)
                grad_right = grad_right + grad
                grad_left = jnp.where(lane == p + i, jnp.sum(grad, 1, keepdims=True), grad_left)
        every = [base + DMAX + j for j in range(GROUP)]
        gk0_ref[...] += transposed_dot(
            beside([[a0_ref[at]] for at in every]),
            beside([[gs_ref[at - d0, mid], gs_ref[at, mid], gs_ref[at + d0, mid]] for at in every]))
        return grad_left, grad_right

    zeros = jnp.zeros((channels, TILE), jnp.float32)
    grad_left, grad_right = lax.fori_loop(0, TILE // GROUP, last, (zeros, zeros))
    gwin_ref[local_row] += 0.5 * grad_left
    gwin_ref[local_row + offset] += 0.5 * grad_right


def tower(tiles, dilation, base_row, window, conv_weight, head_weight, cotangent, total_bins, tile_rows):
    slots = tiles.shape[0]
    channels = window.shape[1]
    blocks = window.shape[0] // TILE
    bf16 = jnp.bfloat16
    f32 = jnp.float32
    window = window.astype(f32)
    left = window[:tile_rows * TILE].reshape(tile_rows, TILE // GROUP, GROUP, channels).transpose(0, 1, 3, 2)
    right = window.reshape(blocks, TILE, channels).transpose(0, 2, 1)
    width = 3 * channels
    taps = 9 * channels
    k0 = conv_weight[0].reshape(taps, channels).T
    k0t = conv_weight[0, ::-1, ::-1].transpose(2, 0, 1, 3).reshape(channels, taps)
    head_f = head_weight.astype(f32)
    folded = jnp.sum(conv_weight[1].astype(f32) * head_f, -1)[::-1, ::-1]
    w1 = jnp.pad(folded, ((0, 0), (0, 13), (0, 0))).transpose(2, 0, 1).reshape(channels, 48).astype(bf16)
    k1 = conv_weight[1].reshape(taps, channels).T
    k1 = jnp.concatenate([jnp.pad(k1, ((0, 0), (0, 48))), jnp.pad(w1, ((0, 0), (taps, 0)))], 0)
    head_b = jnp.broadcast_to(head_f[:, None], (channels, TILE))

    def whole(shape):
        return pl.BlockSpec(shape, lambda s, *_: (0,) * len(shape))

    padded = TILE + 2 * DMAX
    outs = pl.pallas_call(
        partial(tower_kernel, total_bins=total_bins),
        grid_spec=pltpu.PrefetchScalarGridSpec(
            num_scalar_prefetch=3,
            grid=(slots,),
            in_specs=[
                pl.BlockSpec((1, TILE // GROUP, channels, GROUP), lambda s, t, d, b: (t[s] // OFFS, 0, 0, 0)),
                pl.BlockSpec((1, channels, TILE), lambda s, t, d, b: (t[s] // OFFS + t[s] % OFFS, 0, 0)),
                pl.BlockSpec((1, TILE, TILE), lambda s, t, d, b: (s, 0, 0)),
                whole(k0.shape), whole(k1.shape), whole(k0t.shape), whole(head_b.shape),
            ],
            out_specs=[
                pl.BlockSpec((1, TILE, TILE), lambda s, t, d, b: (s, 0, 0)),
                whole((blocks, channels, TILE)),
                whole((3 * channels, 3 * channels)),
                whole((3 * channels, 48)),
                whole((channels, TILE)),
            ],
            scratch_shapes=[
                pltpu.VMEM((padded, width, TILE), bf16),
                pltpu.VMEM((padded, width, TILE), bf16),
                pltpu.VMEM((padded, width, TILE), bf16),
                pltpu.VMEM((padded, 16, TILE), bf16),
                pltpu.VMEM((TILE, channels, TILE), f32),
                pltpu.VMEM((TILE, channels, TILE), f32),
                pltpu.VMEM((width, TILE), f32),
                pltpu.VMEM((TILE, TILE), f32),
                pltpu.VMEM((TILE, TILE), f32),
                pltpu.VMEM((TILE, TILE), f32),
                pltpu.VMEM((TILE, TILE), f32),
            ],
        ),
        out_shape=[
            jax.ShapeDtypeStruct((slots, TILE, TILE), bf16),
            jax.ShapeDtypeStruct((blocks, channels, TILE), f32),
            jax.ShapeDtypeStruct((3 * channels, 3 * channels), f32),
            jax.ShapeDtypeStruct((3 * channels, 48), f32),
            jax.ShapeDtypeStruct((channels, TILE), f32),
        ],
        compiler_params=pltpu.CompilerParams(
            dimension_semantics=("arbitrary",), vmem_limit_bytes=40 * 1024 * 1024),
        name="tower",
    )(tiles, dilation, base_row, left, right, cotangent, k0, k1, k0t, head_b)
    return outs


def steps_of(size):
    steps, low = [], 1
    while low < size:
        span = min(4, size // low)
        steps.append([low * e for e in range(1, span)])
        low *= span
    return steps


def exchange_kernel(
    rows_n, diag_n, tile_rows, per,
    flat_ref, gwin_ref, sum_ref, bins_ref,
    part_ref, got_ref, near_ref, far_ref, own_got, near_got, far_got,
    sum_send, sum_recv, own_send, own_recv, near_send, near_recv, far_send, far_recv,
):
    g = lax.axis_index("rows")
    d = lax.axis_index("diag")
    count = bins_ref.shape[0]
    mesh_id = pl.DeviceIdType.MESH
    steps = [("rows", e) for e in steps_of(rows_n)] + [("diag", e) for e in steps_of(diag_n)]

    def start_of(index):
        return index * per // TILE

    def at(row, diag):
        return {"rows": row, "diag": diag}

    def partner(axis, e):
        return at(g ^ e, d) if axis == "rows" else at(g, d ^ e)

    barrier = pltpu.get_barrier_semaphore()

    def greet(device):
        pl.semaphore_signal(barrier, inc=1, device_id=device, device_id_type=mesh_id)

    met = 0
    for axis, group in steps:
        for e in group:
            greet(partner(axis, e))
            met += 1
    for e in range(1, diag_n):
        greet(at(g, d ^ e))
        met += 1
    firsts = sum(1 for index in range(diag_n) if index * per // TILE == 0)
    for e in range(diag_n):
        @pl.when(g >= 1)
        def _():
            greet(at(g - 1, d ^ e))

        @pl.when((g >= 2) & (start_of(d) == 0))
        def _():
            greet(at(g - 2, d ^ e))
    to_near = 1 - (g + 1) // rows_n
    to_far = 1 - (g + 2) // rows_n
    pl.semaphore_wait(barrier, met + diag_n * to_near + firsts * to_far)

    def remote(src, dst, send, recv, device):
        return pltpu.make_async_remote_copy(
            src_ref=src, dst_ref=dst, send_sem=send, recv_sem=recv,
            device_id=device, device_id_type=mesh_id)

    def sum_copy(step, slot, axis, e):
        src = flat_ref if step == 0 else part_ref.at[step - 1]
        return remote(src, got_ref.at[slot], sum_send.at[slot], sum_recv.at[slot], partner(axis, e))

    def own_copy(e):
        src = gwin_ref.at[pl.ds(start_of(d ^ e), count)]
        return remote(src, own_got.at[e - 1], own_send.at[e - 1], own_recv.at[e - 1], at(g, d ^ e))

    def near_copy(e):
        src = near_ref.at[pl.ds(start_of(d ^ e), count)]
        return remote(src, near_got.at[e], near_send.at[e], near_recv.at[e], at(g + 1, d ^ e))

    def far_copy(e):
        return remote(far_ref, far_got.at[e], far_send.at[e], far_recv.at[e], at(g + 2, d ^ e))

    sends_near = g + 1 < rows_n
    gets_near = g >= 1
    gets_far = (g >= 2) & (start_of(d) == 0)

    def sends_far(e):
        return (g + 2 < rows_n) & (start_of(d ^ e) == 0)

    near_ref[...] = gwin_ref[tile_rows:2 * tile_rows].astype(jnp.bfloat16)
    far_ref[...] = gwin_ref[2 * tile_rows].astype(jnp.bfloat16)
    slot = 0
    value = flat_ref[...]
    copies = []
    for step, (axis, group) in enumerate(steps):
        if step > 0:
            part_ref[step - 1] = value
        here = [sum_copy(step, slot + i, axis, e) for i, e in enumerate(group)]
        for copy in here:
            copy.start()
        if step == 0:
            for e in range(1, diag_n):
                own_copy(e).start()
            for e in range(diag_n):
                pl.when(sends_near)(near_copy(e).start)
                pl.when(sends_far(e))(far_copy(e).start)
        for copy in here:
            copy.wait_recv()
        others = [got_ref[slot + i] for i in range(len(group))]
        value = value + others[0]
        if len(group) == 3:
            value = value + (others[1] + others[2])
        slot += len(group)
        copies += here
    sum_ref[...] = value

    bins_ref[...] = gwin_ref[pl.ds(start_of(d), count)]
    for e in range(1, diag_n):
        own_copy(e).wait_recv()
        bins_ref[...] += own_got[e - 1]

    @pl.when(gets_near)
    def _():
        for e in range(diag_n):
            near_copy(e).wait_recv()
            bins_ref[...] += near_got[e].astype(jnp.float32)

    @pl.when(gets_far)
    def _():
        for e in range(diag_n):
            far_copy(e).wait_recv()
            bins_ref[0] += far_got[e].astype(jnp.float32)

    for copy in copies:
        copy.wait_send()
    for e in range(1, diag_n):
        own_copy(e).wait_send()
    for e in range(diag_n):
        pl.when(sends_near)(near_copy(e).wait_send)
        pl.when(sends_far(e))(far_copy(e).wait_send)


def exchange(flat, gwin, tile_rows):
    rows_n = lax.axis_size("rows")
    diag_n = lax.axis_size("diag")
    per = tile_rows * TILE // diag_n
    count = max(1, per // TILE)
    steps = steps_of(rows_n) + steps_of(diag_n)
    slots = sum(len(group) for group in steps)
    channels = gwin.shape[1]
    block = (channels, TILE)
    f32, bf16 = jnp.float32, jnp.bfloat16
    dma = pltpu.SemaphoreType.DMA
    others = max(1, diag_n - 1)
    vmem = pl.BlockSpec(memory_space=pltpu.VMEM)
    total, bins = pl.pallas_call(
        partial(exchange_kernel, rows_n, diag_n, tile_rows, per),
        out_shape=[jax.ShapeDtypeStruct(flat.shape, f32), jax.ShapeDtypeStruct((count,) + block, f32)],
        in_specs=[vmem] * 2,
        out_specs=[vmem] * 2,
        scratch_shapes=[
            pltpu.VMEM((len(steps),) + flat.shape, f32),
            pltpu.VMEM((slots,) + flat.shape, f32),
            pltpu.VMEM((tile_rows,) + block, bf16),
            pltpu.VMEM(block, bf16),
            pltpu.VMEM((others, count) + block, f32),
            pltpu.VMEM((diag_n, count) + block, bf16),
            pltpu.VMEM((diag_n,) + block, bf16),
            dma((slots,)), dma((slots,)), dma((others,)), dma((others,)),
            dma((diag_n,)), dma((diag_n,)), dma((diag_n,)), dma((diag_n,)),
        ],
        compiler_params=pltpu.CompilerParams(collective_id=0, has_side_effects=True),
        name="exchange",
    )(flat, gwin)
    bins = bins.transpose(0, 2, 1).reshape(count * TILE, channels)
    if per < TILE:
        inside = lax.axis_index("diag") * per % TILE
        bins = lax.dynamic_slice_in_dim(bins, inside, per, 0)
    return total, bins


def on_device(bins, conv_weight, head_weight, dilation, tile_table, cotangent):
    bin_dev = bins.shape[0]
    channels = bins.shape[1]
    tile_rows = bin_dev // TILE
    total_bins = lax.axis_size("rows") * bin_dev
    following = shifted_2(bins, "rows", -1)
    farther = shifted_2(bins[:TILE], "rows", -2)
    window = jnp.concatenate([bins, following, farther], 0)
    base_row = (lax.axis_index("rows") * tile_rows).astype(jnp.int32).reshape(1)
    predicted, gwin, gk0, u1, gh = tower(
        tile_table[0], dilation, base_row, window, conv_weight, head_weight, cotangent[0],
        total_bins, tile_rows)
    width = 3 * channels
    head_sum = jnp.pad(jnp.sum(gh, 1), (0, width - channels))[:, None]
    flat = jnp.concatenate([gk0, u1[:, 1::16], head_sum], 1)
    flat = jnp.pad(flat, ((0, 0), (0, TILE - flat.shape[1])))
    total, grad_bins = exchange(flat, gwin, tile_rows)
    grad_k0 = total[:, :width].reshape(3, channels, 3, channels)[:, :, ::-1].transpose(2, 0, 1, 3)
    u_sum = total[:, width:width + 3].reshape(3, channels, 3)[:, :, ::-1].transpose(2, 0, 1)
    grad_k1 = u_sum[..., None] * head_weight.astype(jnp.float32)
    grad_head = total[:channels, width + 3]
    return (predicted[None], grad_bins, jnp.stack([grad_k0, grad_k1]), grad_head)


def solution(mesh):
    in_specs = (P("rows", None), P(), P(), P(), P("rows", "diag"), P("rows", "diag", None, None))
    out_specs = (P("rows", "diag", None, None), P(("rows", "diag"), None), P(), P())
    return jax.shard_map(
        on_device, mesh=mesh, in_specs=in_specs, out_specs=out_specs, check_vma=False
    )
```

```python
from functools import partial

import jax
import jax.numpy as jnp
from jax import lax
from jax.experimental import pallas as pl
from jax.experimental.pallas import tpu as pltpu
from jax.sharding import PartitionSpec as P

TILE = 128
OFFS = 4
DMAX = 8
BAND = 384
GROUP = 8
OUTSIDE = -1e30


def shifted_2(block, axis, distance):
    devices = range(lax.axis_size(axis))
    route = [(i - distance, i) for i in devices if i - distance in devices]
    return lax.ppermute(block, axis, route)


def shifts(value, spacing, lane):
    before = jnp.where(lane >= spacing, pltpu.roll(value, spacing, 1), 0.0)
    after = jnp.where(lane < TILE - spacing, pltpu.roll(value, TILE - spacing, 1), 0.0)
    return before, value, after


def tower_kernel(
    tiles_ref, dil_ref, base_ref,
    left_ref, right_ref, cot_ref, k0_ref, k1_ref, k0t_ref, head_ref,
    pred_ref, gwin_ref, gk0_ref, u1_ref, gh_ref,
    a0_ref, a1_ref, gs_ref, cs_ref, pair_ref, pair1_ref, right3_ref, cot_f, cot_b, cot_a, pred_f,
    *, total_bins,
):
    step = pl.program_id(0)
    channels = head_ref.shape[0]
    tile_id = tiles_ref[step]
    d0 = dil_ref[0]
    d1 = dil_ref[1]
    local_row = tile_id // OFFS
    offset = tile_id % OFFS

    @pl.when(step == 0)
    def _():
        for ref in (a0_ref, a1_ref, gs_ref, cs_ref):
            edge = jnp.zeros((DMAX,) + ref.shape[1:], ref.dtype)
            ref[:DMAX] = edge
            ref[TILE + DMAX:] = edge
        for ref in (gwin_ref, gk0_ref, u1_ref, gh_ref):
            ref[...] = jnp.zeros_like(ref)

    lane = lax.broadcasted_iota(jnp.int32, (channels, TILE), 1)
    lane_t = lax.broadcasted_iota(jnp.int32, (TILE, TILE), 1)
    sub_t = lax.broadcasted_iota(jnp.int32, (TILE, TILE), 0)
    sub_c = lax.broadcasted_iota(jnp.int32, (16, TILE), 0)
    distance = offset * TILE + lane_t - sub_t
    second = (base_ref[0] + local_row + offset) * TILE + lane_t
    keep = (distance >= 0) & (distance <= BAND) & (second < total_bins)
    masked = jnp.where(keep, cot_ref[0].astype(jnp.float32), 0.0)
    before, _, after = shifts(masked, d1, lane_t)
    cot_f[...] = masked
    cot_b[...] = before
    cot_a[...] = after
    right = right_ref[0]
    right3_ref[:channels] = jnp.where(lane >= d0, pltpu.roll(right, d0, 1), OUTSIDE)
    right3_ref[channels:2 * channels] = right
    right3_ref[2 * channels:] = jnp.where(lane < TILE - d0, pltpu.roll(right, TILE - d0, 1), OUTSIDE)

    def put(ref, p, value, spacing):
        parts = [part.astype(jnp.bfloat16) for part in shifts(value, spacing, lane)]
        ref[p + DMAX] = jnp.concatenate(parts, 0)

    def column(ref, row, spacing):
        return [ref[row - spacing], ref[row], ref[row + spacing]]

    def beside(columns):
        return jnp.concatenate([jnp.concatenate(parts, 0) for parts in columns], 1)

    def transposed_dot(x, y):
        return lax.dot_general(x, y, (((1,), (1,)), ((), ())), preferred_element_type=jnp.float32)

    def slab(ref, base):
        return ref[pl.ds(pl.multiple_of(base, GROUP), GROUP), :]

    def first(g, _):
        base = g * GROUP
        left = left_ref[0, g]
        right3 = right3_ref[...]
        cots = [slab(ref, base) for ref in (cot_b, cot_f, cot_a)]
        ones = [jnp.broadcast_to(left[:, j:j + 1], (channels, TILE)) for j in range(GROUP)]
        for j, one in enumerate(ones):
            p = base + j
            pairs = 0.5 * (jnp.concatenate([one] * 3, 0) + right3)
            pair_ref[p] = pairs[channels:2 * channels]
            a0_ref[p + DMAX] = jnp.maximum(pairs, 0.0).astype(jnp.bfloat16)
            shown = [cot[j:j + 1] for cot in cots]
            row = jnp.where(
                sub_c == 0, shown[0],
                jnp.where(sub_c == 1, shown[1], jnp.where(sub_c == 2, shown[2], 0.0)))
            cs_ref[p + DMAX] = row.astype(jnp.bfloat16)
        return 0

    lax.fori_loop(0, TILE // GROUP, first, 0)

    def second_layer(g, _):
        base = g * GROUP
        values = []
        for j in range(0, GROUP, 2):
            at = base + j + DMAX
            around = beside([column(a0_ref, at + i, d0) for i in range(2)])
            out = jnp.dot(k0_ref[...], around, preferred_element_type=jnp.float32)
            values += [pair_ref[base + j + i] + out[:, i * TILE:(i + 1) * TILE] for i in range(2)]
        for j, value in enumerate(values):
            pair1_ref[base + j] = value
            put(a1_ref, base + j, jnp.maximum(value, 0.0), d1)
        return 0

    lax.fori_loop(0, TILE // GROUP, second_layer, 0)

    head = head_ref[...]

    def turn(g, carry):
        acc_u, acc_h = carry
        base = g * GROUP
        cots = slab(cot_f, base)
        rows, grads = [], []
        for j in range(0, GROUP, 2):
            p = base + j
            at = p + DMAX
            around = beside([column(a1_ref, at + i, d1) + column(cs_ref, at + i, d1) for i in range(2)])
            out = jnp.dot(k1_ref[...], around, preferred_element_type=jnp.float32)
            for i in range(2):
                value = pair1_ref[p + i]
                cot = cots[j + i:j + i + 1]
                pair2 = value + out[:channels, i * TILE:(i + 1) * TILE]
                rows.append(jnp.sum(head * pair2, 0, keepdims=True))
                acc_h = acc_h + pair2 * cot
                grads.append(
                    head * cot + jnp.where(value > 0.0, out[channels:, i * TILE:(i + 1) * TILE], 0.0))
        every = [base + DMAX + j for j in range(GROUP)]
        acc_u = acc_u + transposed_dot(
            beside([[a1_ref[at]] for at in every]), beside([column(cs_ref, at, d1) for at in every]))
        for j, grad in enumerate(grads):
            pair_ref[base + j] = grad
            put(gs_ref, base + j, grad, d0)
        pred_f[pl.ds(pl.multiple_of(base, GROUP), GROUP), :] = jnp.concatenate(rows, 0)
        return acc_u, acc_h

    acc_u, acc_h = lax.fori_loop(
        0, TILE // GROUP, turn, (jnp.zeros(u1_ref.shape, jnp.float32), jnp.zeros(gh_ref.shape, jnp.float32)))
    u1_ref[...] += acc_u
    gh_ref[...] += acc_h
    pred_ref[0] = pred_f[...].astype(jnp.bfloat16)
    mid = slice(channels, 2 * channels)

    def last(g, carry):
        grad_left, grad_right = carry
        base = g * GROUP
        every = [base + DMAX + j for j in range(GROUP)]
        grad_k = transposed_dot(
            beside([[a0_ref[at]] for at in every]),
            beside([[gs_ref[at - d0, mid], gs_ref[at, mid], gs_ref[at + d0, mid]] for at in every]))
        sums = []
        for j in range(0, GROUP, 2):
            p = base + j
            at = p + DMAX
            around = beside([column(gs_ref, at + i, d0) for i in range(2)])
            out = jnp.dot(k0t_ref[...], around, preferred_element_type=jnp.float32)
            for i in range(2):
                active = a0_ref[at + i, mid].astype(jnp.float32) > 0.0
                grad = pair_ref[p + i] + jnp.where(active, out[:, i * TILE:(i + 1) * TILE], 0.0)
                grad_right = grad_right + grad
                sums.append(jnp.sum(grad, 1, keepdims=True))
        for j, total in enumerate(sums):
            grad_left = jnp.where(lane == base + j, total, grad_left)
        gk0_ref[...] += grad_k
        return grad_left, grad_right

    zeros = jnp.zeros((channels, TILE), jnp.float32)
    grad_left, grad_right = lax.fori_loop(0, TILE // GROUP, last, (zeros, zeros))
    gwin_ref[local_row] += 0.5 * grad_left
    gwin_ref[local_row + offset] += 0.5 * grad_right


def tower(tiles, dilation, base_row, window, conv_weight, head_weight, cotangent, total_bins, tile_rows):
    slots = tiles.shape[0]
    channels = window.shape[1]
    blocks = window.shape[0] // TILE
    bf16 = jnp.bfloat16
    f32 = jnp.float32
    window = window.astype(f32)
    left = window[:tile_rows * TILE].reshape(tile_rows, TILE // GROUP, GROUP, channels).transpose(0, 1, 3, 2)
    right = window.reshape(blocks, TILE, channels).transpose(0, 2, 1)
    width = 3 * channels
    taps = 9 * channels
    k0 = conv_weight[0].reshape(taps, channels).T
    k0t = conv_weight[0, ::-1, ::-1].transpose(2, 0, 1, 3).reshape(channels, taps)
    head_f = head_weight.astype(f32)
    folded = jnp.sum(conv_weight[1].astype(f32) * head_f, -1)[::-1, ::-1]
    w1 = jnp.pad(folded, ((0, 0), (0, 13), (0, 0))).transpose(2, 0, 1).reshape(channels, 48).astype(bf16)
    k1 = conv_weight[1].reshape(taps, channels).T
    k1 = jnp.concatenate([jnp.pad(k1, ((0, 0), (0, 48))), jnp.pad(w1, ((0, 0), (taps, 0)))], 0)
    head_b = jnp.broadcast_to(head_f[:, None], (channels, TILE))

    def whole(shape):
        return pl.BlockSpec(shape, lambda s, *_: (0,) * len(shape))

    padded = TILE + 2 * DMAX
    outs = pl.pallas_call(
        partial(tower_kernel, total_bins=total_bins),
        grid_spec=pltpu.PrefetchScalarGridSpec(
            num_scalar_prefetch=3,
            grid=(slots,),
            in_specs=[
                pl.BlockSpec((1, TILE // GROUP, channels, GROUP), lambda s, t, d, b: (t[s] // OFFS, 0, 0, 0)),
                pl.BlockSpec((1, channels, TILE), lambda s, t, d, b: (t[s] // OFFS + t[s] % OFFS, 0, 0)),
                pl.BlockSpec((1, TILE, TILE), lambda s, t, d, b: (s, 0, 0)),
                whole(k0.shape), whole(k1.shape), whole(k0t.shape), whole(head_b.shape),
            ],
            out_specs=[
                pl.BlockSpec((1, TILE, TILE), lambda s, t, d, b: (s, 0, 0)),
                whole((blocks, channels, TILE)),
                whole((3 * channels, 3 * channels)),
                whole((3 * channels, 48)),
                whole((channels, TILE)),
            ],
            scratch_shapes=[
                pltpu.VMEM((padded, width, TILE), bf16),
                pltpu.VMEM((padded, width, TILE), bf16),
                pltpu.VMEM((padded, width, TILE), bf16),
                pltpu.VMEM((padded, 16, TILE), bf16),
                pltpu.VMEM((TILE, channels, TILE), f32),
                pltpu.VMEM((TILE, channels, TILE), f32),
                pltpu.VMEM((width, TILE), f32),
                pltpu.VMEM((TILE, TILE), f32),
                pltpu.VMEM((TILE, TILE), f32),
                pltpu.VMEM((TILE, TILE), f32),
                pltpu.VMEM((TILE, TILE), f32),
            ],
        ),
        out_shape=[
            jax.ShapeDtypeStruct((slots, TILE, TILE), bf16),
            jax.ShapeDtypeStruct((blocks, channels, TILE), f32),
            jax.ShapeDtypeStruct((3 * channels, 3 * channels), f32),
            jax.ShapeDtypeStruct((3 * channels, 48), f32),
            jax.ShapeDtypeStruct((channels, TILE), f32),
        ],
        compiler_params=pltpu.CompilerParams(
            dimension_semantics=("arbitrary",), vmem_limit_bytes=40 * 1024 * 1024),
        name="tower",
    )(tiles, dilation, base_row, left, right, cotangent, k0, k1, k0t, head_b)
    return outs


def steps_of(size):
    steps, low = [], 1
    while low < size:
        span = min(4, size // low)
        steps.append([low * e for e in range(1, span)])
        low *= span
    return steps


def exchange_kernel(
    rows_n, diag_n, tile_rows, per,
    flat_ref, gwin_ref, sum_ref, bins_ref,
    part_ref, got_ref, near_ref, far_ref, own_got, near_got, far_got,
    sum_send, sum_recv, own_send, own_recv, near_send, near_recv, far_send, far_recv,
):
    g = lax.axis_index("rows")
    d = lax.axis_index("diag")
    count = bins_ref.shape[0]
    mesh_id = pl.DeviceIdType.MESH
    steps = [("rows", e) for e in steps_of(rows_n)] + [("diag", e) for e in steps_of(diag_n)]

    def start_of(index):
        return index * per // TILE

    def at(row, diag):
        return {"rows": row, "diag": diag}

    def partner(axis, e):
        return at(g ^ e, d) if axis == "rows" else at(g, d ^ e)

    barrier = pltpu.get_barrier_semaphore()

    def greet(device):
        pl.semaphore_signal(barrier, inc=1, device_id=device, device_id_type=mesh_id)

    met = 0
    for axis, group in steps:
        for e in group:
            greet(partner(axis, e))
            met += 1
    for e in range(1, diag_n):
        greet(at(g, d ^ e))
        met += 1
    firsts = sum(1 for index in range(diag_n) if index * per // TILE == 0)
    for e in range(diag_n):
        @pl.when(g >= 1)
        def _():
            greet(at(g - 1, d ^ e))

        @pl.when((g >= 2) & (start_of(d) == 0))
        def _():
            greet(at(g - 2, d ^ e))
    to_near = 1 - (g + 1) // rows_n
    to_far = 1 - (g + 2) // rows_n
    pl.semaphore_wait(barrier, met + diag_n * to_near + firsts * to_far)

    def remote(src, dst, send, recv, device):
        return pltpu.make_async_remote_copy(
            src_ref=src, dst_ref=dst, send_sem=send, recv_sem=recv,
            device_id=device, device_id_type=mesh_id)

    def sum_copy(step, slot, axis, e):
        src = flat_ref if step == 0 else part_ref.at[step - 1]
        return remote(src, got_ref.at[slot], sum_send.at[slot], sum_recv.at[slot], partner(axis, e))

    def own_copy(e):
        src = gwin_ref.at[pl.ds(start_of(d ^ e), count)]
        return remote(src, own_got.at[e - 1], own_send.at[e - 1], own_recv.at[e - 1], at(g, d ^ e))

    def near_copy(e):
        src = near_ref.at[pl.ds(start_of(d ^ e), count)]
        return remote(src, near_got.at[e], near_send.at[e], near_recv.at[e], at(g + 1, d ^ e))

    def far_copy(e):
        return remote(far_ref, far_got.at[e], far_send.at[e], far_recv.at[e], at(g + 2, d ^ e))

    sends_near = g + 1 < rows_n
    gets_near = g >= 1
    gets_far = (g >= 2) & (start_of(d) == 0)

    def sends_far(e):
        return (g + 2 < rows_n) & (start_of(d ^ e) == 0)

    near_ref[...] = gwin_ref[tile_rows:2 * tile_rows].astype(jnp.bfloat16)
    far_ref[...] = gwin_ref[2 * tile_rows].astype(jnp.bfloat16)
    slot = 0
    value = flat_ref[...]
    copies = []
    for step, (axis, group) in enumerate(steps):
        if step > 0:
            part_ref[step - 1] = value
        here = [sum_copy(step, slot + i, axis, e) for i, e in enumerate(group)]
        for copy in here:
            copy.start()
        if step == 0:
            for e in range(1, diag_n):
                own_copy(e).start()
            for e in range(diag_n):
                pl.when(sends_near)(near_copy(e).start)
                pl.when(sends_far(e))(far_copy(e).start)
        for copy in here:
            copy.wait_recv()
        others = [got_ref[slot + i] for i in range(len(group))]
        value = value + others[0]
        if len(group) == 3:
            value = value + (others[1] + others[2])
        slot += len(group)
        copies += here
    sum_ref[...] = value

    bins_ref[...] = gwin_ref[pl.ds(start_of(d), count)]
    for e in range(1, diag_n):
        own_copy(e).wait_recv()
        bins_ref[...] += own_got[e - 1]

    @pl.when(gets_near)
    def _():
        for e in range(diag_n):
            near_copy(e).wait_recv()
            bins_ref[...] += near_got[e].astype(jnp.float32)

    @pl.when(gets_far)
    def _():
        for e in range(diag_n):
            far_copy(e).wait_recv()
            bins_ref[0] += far_got[e].astype(jnp.float32)

    for copy in copies:
        copy.wait_send()
    for e in range(1, diag_n):
        own_copy(e).wait_send()
    for e in range(diag_n):
        pl.when(sends_near)(near_copy(e).wait_send)
        pl.when(sends_far(e))(far_copy(e).wait_send)


def exchange(flat, gwin, tile_rows):
    rows_n = lax.axis_size("rows")
    diag_n = lax.axis_size("diag")
    per = tile_rows * TILE // diag_n
    count = max(1, per // TILE)
    steps = steps_of(rows_n) + steps_of(diag_n)
    slots = sum(len(group) for group in steps)
    channels = gwin.shape[1]
    block = (channels, TILE)
    f32, bf16 = jnp.float32, jnp.bfloat16
    dma = pltpu.SemaphoreType.DMA
    others = max(1, diag_n - 1)
    vmem = pl.BlockSpec(memory_space=pltpu.VMEM)
    total, bins = pl.pallas_call(
        partial(exchange_kernel, rows_n, diag_n, tile_rows, per),
        out_shape=[jax.ShapeDtypeStruct(flat.shape, f32), jax.ShapeDtypeStruct((count,) + block, f32)],
        in_specs=[vmem] * 2,
        out_specs=[vmem] * 2,
        scratch_shapes=[
            pltpu.VMEM((len(steps),) + flat.shape, f32),
            pltpu.VMEM((slots,) + flat.shape, f32),
            pltpu.VMEM((tile_rows,) + block, bf16),
            pltpu.VMEM(block, bf16),
            pltpu.VMEM((others, count) + block, f32),
            pltpu.VMEM((diag_n, count) + block, bf16),
            pltpu.VMEM((diag_n,) + block, bf16),
            dma((slots,)), dma((slots,)), dma((others,)), dma((others,)),
            dma((diag_n,)), dma((diag_n,)), dma((diag_n,)), dma((diag_n,)),
        ],
        compiler_params=pltpu.CompilerParams(collective_id=0, has_side_effects=True),
        name="exchange",
    )(flat, gwin)
    bins = bins.transpose(0, 2, 1).reshape(count * TILE, channels)
    if per < TILE:
        inside = lax.axis_index("diag") * per % TILE
        bins = lax.dynamic_slice_in_dim(bins, inside, per, 0)
    return total, bins


def on_device(bins, conv_weight, head_weight, dilation, tile_table, cotangent):
    bin_dev = bins.shape[0]
    channels = bins.shape[1]
    tile_rows = bin_dev // TILE
    total_bins = lax.axis_size("rows") * bin_dev
    following = shifted_2(bins, "rows", -1)
    farther = shifted_2(bins[:TILE], "rows", -2)
    window = jnp.concatenate([bins, following, farther], 0)
    base_row = (lax.axis_index("rows") * tile_rows).astype(jnp.int32).reshape(1)
    predicted, gwin, gk0, u1, gh = tower(
        tile_table[0], dilation, base_row, window, conv_weight, head_weight, cotangent[0],
        total_bins, tile_rows)
    width = 3 * channels
    head_sum = jnp.pad(jnp.sum(gh, 1), (0, width - channels))[:, None]
    flat = jnp.concatenate([gk0, u1[:, 1::16], head_sum], 1)
    flat = jnp.pad(flat, ((0, 0), (0, TILE - flat.shape[1])))
    total, grad_bins = exchange(flat, gwin, tile_rows)
    grad_k0 = total[:, :width].reshape(3, channels, 3, channels)[:, :, ::-1].transpose(2, 0, 1, 3)
    u_sum = total[:, width:width + 3].reshape(3, channels, 3)[:, :, ::-1].transpose(2, 0, 1)
    grad_k1 = u_sum[..., None] * head_weight.astype(jnp.float32)
    grad_head = total[:channels, width + 3]
    return (predicted[None], grad_bins, jnp.stack([grad_k0, grad_k1]), grad_head)


def solution(mesh):
    in_specs = (P("rows", None), P(), P(), P(), P("rows", "diag"), P("rows", "diag", None, None))
    out_specs = (P("rows", "diag", None, None), P(("rows", "diag"), None), P(), P())
    return jax.shard_map(
        on_device, mesh=mesh, in_specs=in_specs, out_specs=out_specs, check_vma=False
    )
```

```python
from functools import partial

import jax
import jax.numpy as jnp
from jax import lax
from jax.experimental import pallas as pl
from jax.experimental.pallas import tpu as pltpu
from jax.sharding import PartitionSpec as P

TILE = 128
OFFS = 4
DMAX = 8
BAND = 384
GROUP = 8
OUTSIDE = -1e30


def shifted_2(block, axis, distance):
    devices = range(lax.axis_size(axis))
    route = [(i - distance, i) for i in devices if i - distance in devices]
    return lax.ppermute(block, axis, route)


def shifts(value, spacing, lane):
    before = jnp.where(lane >= spacing, pltpu.roll(value, spacing, 1), 0.0)
    after = jnp.where(lane < TILE - spacing, pltpu.roll(value, TILE - spacing, 1), 0.0)
    return before, value, after


def tower_kernel(
    tiles_ref, dil_ref, base_ref,
    left_ref, right_ref, cot_ref, k0_ref, k0n_ref, k1_ref, k1n_ref, k0t_ref, k0tn_ref, w1_ref, head_ref,
    pred_ref, gwin_ref, gk0_ref, u1_ref, gh_ref,
    a0_ref, a1_ref, gs_ref, cs_ref, pair_ref, pair1_ref, right3_ref, cot_f, cot_b, cot_a, pred_f,
    *, total_bins,
):
    step = pl.program_id(0)
    channels = head_ref.shape[0]
    tile_id = tiles_ref[step]
    d0 = dil_ref[0]
    d1 = dil_ref[1]
    local_row = tile_id // OFFS
    offset = tile_id % OFFS

    @pl.when(step == 0)
    def _():
        for ref in (a0_ref, a1_ref, gs_ref, cs_ref):
            edge = jnp.zeros((DMAX,) + ref.shape[1:], ref.dtype)
            ref[:DMAX] = edge
            ref[TILE + DMAX:] = edge
        for ref in (gwin_ref, gk0_ref, u1_ref, gh_ref):
            ref[...] = jnp.zeros_like(ref)

    lane = lax.broadcasted_iota(jnp.int32, (channels, TILE), 1)
    lane_t = lax.broadcasted_iota(jnp.int32, (TILE, TILE), 1)
    sub_t = lax.broadcasted_iota(jnp.int32, (TILE, TILE), 0)
    sub_c = lax.broadcasted_iota(jnp.int32, (16, TILE), 0)
    distance = offset * TILE + lane_t - sub_t
    second = (base_ref[0] + local_row + offset) * TILE + lane_t
    keep = (distance >= 0) & (distance <= BAND) & (second < total_bins)
    masked = jnp.where(keep, cot_ref[0].astype(jnp.float32), 0.0)
    before, _, after = shifts(masked, d1, lane_t)
    cot_f[...] = masked
    cot_b[...] = before
    cot_a[...] = after
    right = right_ref[0]
    right3_ref[:channels] = jnp.where(lane >= d0, pltpu.roll(right, d0, 1), OUTSIDE)
    right3_ref[channels:2 * channels] = right
    right3_ref[2 * channels:] = jnp.where(lane < TILE - d0, pltpu.roll(right, TILE - d0, 1), OUTSIDE)

    def put(ref, p, value, spacing):
        parts = [part.astype(jnp.bfloat16) for part in shifts(value, spacing, lane)]
        ref[p + DMAX] = jnp.concatenate(parts, 0)

    def column(ref, row, spacing):
        return [ref[row - spacing], ref[row], ref[row + spacing]]

    def beside(columns):
        return jnp.concatenate([jnp.concatenate(parts, 0) for parts in columns], 1)

    def transposed_dot(x, y):
        return lax.dot_general(x, y, (((1,), (1,)), ((), ())), preferred_element_type=jnp.float32)

    def heads_of(ref, base, spacing):
        heads, ninth = [], []
        for j in range(0, GROUP, 2):
            rows = [base + DMAX + j + i for i in range(2)]
            heads.append(beside([
                [ref[at - spacing], ref[at], ref[at + spacing, :2 * channels]] for at in rows]))
            ninth.append(beside([[ref[at + spacing, 2 * channels:]] for at in rows]))
        return heads, jnp.concatenate(ninth, 0)

    def taps_of(ref, base, spacing, kernel_ref, ninth_ref):
        heads, ninth = heads_of(ref, base, spacing)
        rest = jnp.dot(ninth_ref[...], ninth, preferred_element_type=jnp.float32)
        return [
            rest[k * channels:(k + 1) * channels]
            + jnp.dot(kernel_ref[...], part, preferred_element_type=jnp.float32)
            for k, part in enumerate(heads)]

    def first(g, _):
        left = left_ref[0, g]
        for j in range(GROUP):
            p = g * GROUP + j
            one = jnp.broadcast_to(left[:, j:j + 1], (channels, TILE))
            pairs = 0.5 * (jnp.concatenate([one] * 3, 0) + right3_ref[...])
            pair_ref[p] = pairs[channels:2 * channels]
            a0_ref[p + DMAX] = jnp.maximum(pairs, 0.0).astype(jnp.bfloat16)
            row = jnp.where(
                sub_c == 0, cot_b[pl.ds(p, 1), :],
                jnp.where(sub_c == 1, cot_f[pl.ds(p, 1), :],
                          jnp.where(sub_c == 2, cot_a[pl.ds(p, 1), :], 0.0)))
            cs_ref[p + DMAX] = row.astype(jnp.bfloat16)
        return 0

    lax.fori_loop(0, TILE // GROUP, first, 0)

    def second_layer(g, _):
        outs = taps_of(a0_ref, g * GROUP, d0, k0_ref, k0n_ref)
        for j in range(0, GROUP, 2):
            p = g * GROUP + j
            out = outs[j // 2]
            for i in range(2):
                value = pair_ref[p + i] + out[:, i * TILE:(i + 1) * TILE]
                pair1_ref[p + i] = value
                put(a1_ref, p + i, jnp.maximum(value, 0.0), d1)
        return 0

    lax.fori_loop(0, TILE // GROUP, second_layer, 0)

    head = head_ref[...]

    def turn(g, carry):
        acc_u, acc_h = carry
        base = g * GROUP
        rows = []
        outs = taps_of(a1_ref, base, d1, k1_ref, k1n_ref)
        cots = jnp.concatenate([
            beside([column(cs_ref, base + DMAX + j + i, d1) for i in range(2)])
            for j in range(0, GROUP, 2)], 0)
        backs = jnp.dot(w1_ref[...], cots, preferred_element_type=jnp.float32)
        for j in range(0, GROUP, 2):
            p = base + j
            out = outs[j // 2]
            back = backs[j // 2 * channels:(j // 2 + 1) * channels]
            for i in range(2):
                value = pair1_ref[p + i]
                cot = cot_f[pl.ds(p + i, 1), :]
                pair2 = value + out[:, i * TILE:(i + 1) * TILE]
                rows.append(jnp.sum(head * pair2, 0, keepdims=True))
                acc_h = acc_h + pair2 * cot
                grad = head * cot + jnp.where(value > 0.0, back[:, i * TILE:(i + 1) * TILE], 0.0)
                pair_ref[p + i] = grad
                put(gs_ref, p + i, grad, d0)
        pred_f[pl.ds(pl.multiple_of(base, GROUP), GROUP), :] = jnp.concatenate(rows, 0)
        every = [base + DMAX + j for j in range(GROUP)]
        acc_u = acc_u + transposed_dot(
            beside([[a1_ref[at]] for at in every]), beside([column(cs_ref, at, d1) for at in every]))
        return acc_u, acc_h

    acc_u, acc_h = lax.fori_loop(
        0, TILE // GROUP, turn, (jnp.zeros(u1_ref.shape, jnp.float32), jnp.zeros(gh_ref.shape, jnp.float32)))
    u1_ref[...] += acc_u
    gh_ref[...] += acc_h
    pred_ref[0] = pred_f[...].astype(jnp.bfloat16)
    mid = slice(channels, 2 * channels)

    def last(g, carry):
        grad_left, grad_right = carry
        base = g * GROUP
        outs = taps_of(gs_ref, base, d0, k0t_ref, k0tn_ref)
        for j in range(0, GROUP, 2):
            p = base + j
            at = p + DMAX
            out = outs[j // 2]
            for i in range(2):
                active = a0_ref[at + i, mid].astype(jnp.float32) > 0.0
                grad = pair_ref[p + i] + jnp.where(active, out[:, i * TILE:(i + 1) * TILE], 0.0)
                grad_right = grad_right + grad
                grad_left = jnp.where(lane == p + i, jnp.sum(grad, 1, keepdims=True), grad_left)
        every = [base + DMAX + j for j in range(GROUP)]
        gk0_ref[...] += transposed_dot(
            beside([[a0_ref[at]] for at in every]),
            beside([[gs_ref[at - d0, mid], gs_ref[at, mid], gs_ref[at + d0, mid]] for at in every]))
        return grad_left, grad_right

    zeros = jnp.zeros((channels, TILE), jnp.float32)
    grad_left, grad_right = lax.fori_loop(0, TILE // GROUP, last, (zeros, zeros))
    gwin_ref[local_row] += 0.5 * grad_left
    gwin_ref[local_row + offset] += 0.5 * grad_right


def tower(tiles, dilation, base_row, window, conv_weight, head_weight, cotangent, total_bins, tile_rows):
    slots = tiles.shape[0]
    channels = window.shape[1]
    blocks = window.shape[0] // TILE
    bf16 = jnp.bfloat16
    f32 = jnp.float32
    window = window.astype(f32)
    left = window[:tile_rows * TILE].reshape(tile_rows, TILE // GROUP, GROUP, channels).transpose(0, 1, 3, 2)
    right = window.reshape(blocks, TILE, channels).transpose(0, 2, 1)
    width = 3 * channels
    taps = 9 * channels
    k0 = conv_weight[0].reshape(taps, channels).T
    k0t = conv_weight[0, ::-1, ::-1].transpose(2, 0, 1, 3).reshape(channels, taps)
    head_f = head_weight.astype(f32)
    folded = jnp.sum(conv_weight[1].astype(f32) * head_f, -1)[::-1, ::-1]
    w1 = jnp.pad(folded, ((0, 0), (0, 13), (0, 0))).transpose(2, 0, 1).reshape(channels, 48).astype(bf16)
    k1 = conv_weight[1].reshape(taps, channels).T
    repeat = jnp.eye(GROUP // 2, dtype=bf16)

    def diagonal(block):
        size = (GROUP // 2 * block.shape[0], GROUP // 2 * block.shape[1])
        return (repeat[:, None, :, None] * block[None, :, None, :]).reshape(size)

    kernels = []
    for kernel in (k0, k1, k0t):
        kernels += [kernel[:, :8 * channels], diagonal(kernel[:, 8 * channels:])]
    kernels += [diagonal(w1), jnp.broadcast_to(head_f[:, None], (channels, TILE))]

    def whole(shape):
        return pl.BlockSpec(shape, lambda s, *_: (0,) * len(shape))

    padded = TILE + 2 * DMAX
    outs = pl.pallas_call(
        partial(tower_kernel, total_bins=total_bins),
        grid_spec=pltpu.PrefetchScalarGridSpec(
            num_scalar_prefetch=3,
            grid=(slots,),
            in_specs=[
                pl.BlockSpec((1, TILE // GROUP, channels, GROUP), lambda s, t, d, b: (t[s] // OFFS, 0, 0, 0)),
                pl.BlockSpec((1, channels, TILE), lambda s, t, d, b: (t[s] // OFFS + t[s] % OFFS, 0, 0)),
                pl.BlockSpec((1, TILE, TILE), lambda s, t, d, b: (s, 0, 0)),
                *[whole(kernel.shape) for kernel in kernels],
            ],
            out_specs=[
                pl.BlockSpec((1, TILE, TILE), lambda s, t, d, b: (s, 0, 0)),
                whole((blocks, channels, TILE)),
                whole((3 * channels, 3 * channels)),
                whole((3 * channels, 48)),
                whole((channels, TILE)),
            ],
            scratch_shapes=[
                pltpu.VMEM((padded, width, TILE), bf16),
                pltpu.VMEM((padded, width, TILE), bf16),
                pltpu.VMEM((padded, width, TILE), bf16),
                pltpu.VMEM((padded, 16, TILE), bf16),
                pltpu.VMEM((TILE, channels, TILE), f32),
                pltpu.VMEM((TILE, channels, TILE), f32),
                pltpu.VMEM((width, TILE), f32),
                pltpu.VMEM((TILE, TILE), f32),
                pltpu.VMEM((TILE, TILE), f32),
                pltpu.VMEM((TILE, TILE), f32),
                pltpu.VMEM((TILE, TILE), f32),
            ],
        ),
        out_shape=[
            jax.ShapeDtypeStruct((slots, TILE, TILE), bf16),
            jax.ShapeDtypeStruct((blocks, channels, TILE), f32),
            jax.ShapeDtypeStruct((3 * channels, 3 * channels), f32),
            jax.ShapeDtypeStruct((3 * channels, 48), f32),
            jax.ShapeDtypeStruct((channels, TILE), f32),
        ],
        compiler_params=pltpu.CompilerParams(
            dimension_semantics=("arbitrary",), vmem_limit_bytes=40 * 1024 * 1024),
        name="tower",
    )(tiles, dilation, base_row, left, right, cotangent, *kernels)
    return outs


def steps_of(size):
    steps, low = [], 1
    while low < size:
        span = min(4, size // low)
        steps.append([low * e for e in range(1, span)])
        low *= span
    return steps


def exchange_kernel(
    rows_n, diag_n, tile_rows, per,
    flat_ref, gwin_ref, sum_ref, bins_ref,
    part_ref, got_ref, near_ref, far_ref, own_got, near_got, far_got,
    sum_send, sum_recv, own_send, own_recv, near_send, near_recv, far_send, far_recv,
):
    g = lax.axis_index("rows")
    d = lax.axis_index("diag")
    count = bins_ref.shape[0]
    mesh_id = pl.DeviceIdType.MESH
    steps = [("rows", e) for e in steps_of(rows_n)] + [("diag", e) for e in steps_of(diag_n)]

    def start_of(index):
        return index * per // TILE

    def at(row, diag):
        return {"rows": row, "diag": diag}

    def partner(axis, e):
        return at(g ^ e, d) if axis == "rows" else at(g, d ^ e)

    barrier = pltpu.get_barrier_semaphore()

    def greet(device):
        pl.semaphore_signal(barrier, inc=1, device_id=device, device_id_type=mesh_id)

    met = 0
    for axis, group in steps:
        for e in group:
            greet(partner(axis, e))
            met += 1
    for e in range(1, diag_n):
        greet(at(g, d ^ e))
        met += 1
    firsts = sum(1 for index in range(diag_n) if index * per // TILE == 0)
    for e in range(diag_n):
        @pl.when(g >= 1)
        def _():
            greet(at(g - 1, d ^ e))

        @pl.when((g >= 2) & (start_of(d) == 0))
        def _():
            greet(at(g - 2, d ^ e))
    to_near = 1 - (g + 1) // rows_n
    to_far = 1 - (g + 2) // rows_n
    pl.semaphore_wait(barrier, met + diag_n * to_near + firsts * to_far)

    def remote(src, dst, send, recv, device):
        return pltpu.make_async_remote_copy(
            src_ref=src, dst_ref=dst, send_sem=send, recv_sem=recv,
            device_id=device, device_id_type=mesh_id)

    def sum_copy(step, slot, axis, e):
        src = flat_ref if step == 0 else part_ref.at[step - 1]
        return remote(src, got_ref.at[slot], sum_send.at[slot], sum_recv.at[slot], partner(axis, e))

    def own_copy(e):
        src = gwin_ref.at[pl.ds(start_of(d ^ e), count)]
        return remote(src, own_got.at[e - 1], own_send.at[e - 1], own_recv.at[e - 1], at(g, d ^ e))

    def near_copy(e):
        src = near_ref.at[pl.ds(start_of(d ^ e), count)]
        return remote(src, near_got.at[e], near_send.at[e], near_recv.at[e], at(g + 1, d ^ e))

    def far_copy(e):
        return remote(far_ref, far_got.at[e], far_send.at[e], far_recv.at[e], at(g + 2, d ^ e))

    sends_near = g + 1 < rows_n
    gets_near = g >= 1
    gets_far = (g >= 2) & (start_of(d) == 0)

    def sends_far(e):
        return (g + 2 < rows_n) & (start_of(d ^ e) == 0)

    near_ref[...] = gwin_ref[tile_rows:2 * tile_rows].astype(jnp.bfloat16)
    far_ref[...] = gwin_ref[2 * tile_rows].astype(jnp.bfloat16)
    slot = 0
    value = flat_ref[...]
    copies = []
    for step, (axis, group) in enumerate(steps):
        if step > 0:
            part_ref[step - 1] = value
        here = [sum_copy(step, slot + i, axis, e) for i, e in enumerate(group)]
        for copy in here:
            copy.start()
        if step == 0:
            for e in range(1, diag_n):
                own_copy(e).start()
            for e in range(diag_n):
                pl.when(sends_near)(near_copy(e).start)
                pl.when(sends_far(e))(far_copy(e).start)
        for copy in here:
            copy.wait_recv()
        others = [got_ref[slot + i] for i in range(len(group))]
        value = value + others[0]
        if len(group) == 3:
            value = value + (others[1] + others[2])
        slot += len(group)
        copies += here
    sum_ref[...] = value

    bins_ref[...] = gwin_ref[pl.ds(start_of(d), count)]
    for e in range(1, diag_n):
        own_copy(e).wait_recv()
        bins_ref[...] += own_got[e - 1]

    @pl.when(gets_near)
    def _():
        for e in range(diag_n):
            near_copy(e).wait_recv()
            bins_ref[...] += near_got[e].astype(jnp.float32)

    @pl.when(gets_far)
    def _():
        for e in range(diag_n):
            far_copy(e).wait_recv()
            bins_ref[0] += far_got[e].astype(jnp.float32)

    for copy in copies:
        copy.wait_send()
    for e in range(1, diag_n):
        own_copy(e).wait_send()
    for e in range(diag_n):
        pl.when(sends_near)(near_copy(e).wait_send)
        pl.when(sends_far(e))(far_copy(e).wait_send)


def exchange(flat, gwin, tile_rows):
    rows_n = lax.axis_size("rows")
    diag_n = lax.axis_size("diag")
    per = tile_rows * TILE // diag_n
    count = max(1, per // TILE)
    steps = steps_of(rows_n) + steps_of(diag_n)
    slots = sum(len(group) for group in steps)
    channels = gwin.shape[1]
    block = (channels, TILE)
    f32, bf16 = jnp.float32, jnp.bfloat16
    dma = pltpu.SemaphoreType.DMA
    others = max(1, diag_n - 1)
    vmem = pl.BlockSpec(memory_space=pltpu.VMEM)
    total, bins = pl.pallas_call(
        partial(exchange_kernel, rows_n, diag_n, tile_rows, per),
        out_shape=[jax.ShapeDtypeStruct(flat.shape, f32), jax.ShapeDtypeStruct((count,) + block, f32)],
        in_specs=[vmem] * 2,
        out_specs=[vmem] * 2,
        scratch_shapes=[
            pltpu.VMEM((len(steps),) + flat.shape, f32),
            pltpu.VMEM((slots,) + flat.shape, f32),
            pltpu.VMEM((tile_rows,) + block, bf16),
            pltpu.VMEM(block, bf16),
            pltpu.VMEM((others, count) + block, f32),
            pltpu.VMEM((diag_n, count) + block, bf16),
            pltpu.VMEM((diag_n,) + block, bf16),
            dma((slots,)), dma((slots,)), dma((others,)), dma((others,)),
            dma((diag_n,)), dma((diag_n,)), dma((diag_n,)), dma((diag_n,)),
        ],
        compiler_params=pltpu.CompilerParams(collective_id=0, has_side_effects=True),
        name="exchange",
    )(flat, gwin)
    bins = bins.transpose(0, 2, 1).reshape(count * TILE, channels)
    if per < TILE:
        inside = lax.axis_index("diag") * per % TILE
        bins = lax.dynamic_slice_in_dim(bins, inside, per, 0)
    return total, bins


def on_device(bins, conv_weight, head_weight, dilation, tile_table, cotangent):
    bin_dev = bins.shape[0]
    channels = bins.shape[1]
    tile_rows = bin_dev // TILE
    total_bins = lax.axis_size("rows") * bin_dev
    following = shifted_2(bins, "rows", -1)
    farther = shifted_2(bins[:TILE], "rows", -2)
    window = jnp.concatenate([bins, following, farther], 0)
    base_row = (lax.axis_index("rows") * tile_rows).astype(jnp.int32).reshape(1)
    predicted, gwin, gk0, u1, gh = tower(
        tile_table[0], dilation, base_row, window, conv_weight, head_weight, cotangent[0],
        total_bins, tile_rows)
    width = 3 * channels
    head_sum = jnp.pad(jnp.sum(gh, 1), (0, width - channels))[:, None]
    flat = jnp.concatenate([gk0, u1[:, 1::16], head_sum], 1)
    flat = jnp.pad(flat, ((0, 0), (0, TILE - flat.shape[1])))
    total, grad_bins = exchange(flat, gwin, tile_rows)
    grad_k0 = total[:, :width].reshape(3, channels, 3, channels)[:, :, ::-1].transpose(2, 0, 1, 3)
    u_sum = total[:, width:width + 3].reshape(3, channels, 3)[:, :, ::-1].transpose(2, 0, 1)
    grad_k1 = u_sum[..., None] * head_weight.astype(jnp.float32)
    grad_head = total[:channels, width + 3]
    return (predicted[None], grad_bins, jnp.stack([grad_k0, grad_k1]), grad_head)


def solution(mesh):
    in_specs = (P("rows", None), P(), P(), P(), P("rows", "diag"), P("rows", "diag", None, None))
    out_specs = (P("rows", "diag", None, None), P(("rows", "diag"), None), P(), P())
    return jax.shard_map(
        on_device, mesh=mesh, in_specs=in_specs, out_specs=out_specs, check_vma=False
    )
```

```python
from functools import partial

import jax
import jax.numpy as jnp
from jax import lax
from jax.experimental import pallas as pl
from jax.experimental.pallas import tpu as pltpu
from jax.sharding import PartitionSpec as P

TILE = 128
OFFS = 4
DMAX = 8
BAND = 384
GROUP = 8
OUTSIDE = -1e30


def shifted_2(block, axis, distance):
    devices = range(lax.axis_size(axis))
    route = [(i - distance, i) for i in devices if i - distance in devices]
    return lax.ppermute(block, axis, route)


def shifts(value, spacing, lane):
    before = jnp.where(lane >= spacing, pltpu.roll(value, spacing, 1), 0.0)
    after = jnp.where(lane < TILE - spacing, pltpu.roll(value, TILE - spacing, 1), 0.0)
    return before, value, after


def tower_kernel(
    tiles_ref, dil_ref, base_ref,
    left_ref, right_ref, cot_ref, k0_ref, k0n_ref, k1_ref, k1n_ref, k0t_ref, k0tn_ref, w1_ref, head_ref,
    pred_ref, gwin_ref, gk0_ref, u1_ref, gh_ref,
    a0_ref, a1_ref, gs_ref, cs_ref, pair_ref, pair1_ref, right3_ref, cot_f, cot_b, cot_a, pred_f,
    *, total_bins,
):
    step = pl.program_id(0)
    channels = head_ref.shape[0]
    tile_id = tiles_ref[step]
    d0 = dil_ref[0]
    d1 = dil_ref[1]
    local_row = tile_id // OFFS
    offset = tile_id % OFFS

    @pl.when(step == 0)
    def _():
        for ref in (a0_ref, a1_ref, gs_ref, cs_ref):
            edge = jnp.zeros((DMAX,) + ref.shape[1:], ref.dtype)
            ref[:DMAX] = edge
            ref[TILE + DMAX:] = edge
        for ref in (gwin_ref, gk0_ref, u1_ref, gh_ref):
            ref[...] = jnp.zeros_like(ref)

    lane = lax.broadcasted_iota(jnp.int32, (channels, TILE), 1)
    lane_t = lax.broadcasted_iota(jnp.int32, (TILE, TILE), 1)
    sub_t = lax.broadcasted_iota(jnp.int32, (TILE, TILE), 0)
    sub_c = lax.broadcasted_iota(jnp.int32, (16, TILE), 0)
    distance = offset * TILE + lane_t - sub_t
    second = (base_ref[0] + local_row + offset) * TILE + lane_t
    keep = (distance >= 0) & (distance <= BAND) & (second < total_bins)
    masked = jnp.where(keep, cot_ref[0].astype(jnp.float32), 0.0)
    before, _, after = shifts(masked, d1, lane_t)
    cot_f[...] = masked
    cot_b[...] = before
    cot_a[...] = after
    right = right_ref[0]
    right3_ref[:channels] = jnp.where(lane >= d0, pltpu.roll(right, d0, 1), OUTSIDE)
    right3_ref[channels:2 * channels] = right
    right3_ref[2 * channels:] = jnp.where(lane < TILE - d0, pltpu.roll(right, TILE - d0, 1), OUTSIDE)

    def put(ref, p, value, spacing):
        parts = [part.astype(jnp.bfloat16) for part in shifts(value, spacing, lane)]
        ref[p + DMAX] = jnp.concatenate(parts, 0)

    def column(ref, row, spacing):
        return [ref[row - spacing], ref[row], ref[row + spacing]]

    def beside(columns):
        return jnp.concatenate([jnp.concatenate(parts, 0) for parts in columns], 1)

    def transposed_dot(x, y):
        return lax.dot_general(x, y, (((1,), (1,)), ((), ())), preferred_element_type=jnp.float32)

    def heads_of(ref, base, spacing):
        heads, ninth = [], []
        for j in range(0, GROUP, 2):
            rows = [base + DMAX + j + i for i in range(2)]
            heads.append(beside([
                [ref[at - spacing], ref[at], ref[at + spacing, :2 * channels]] for at in rows]))
            ninth.append(beside([[ref[at + spacing, 2 * channels:]] for at in rows]))
        return heads, jnp.concatenate(ninth, 0)

    def taps_of(ref, base, spacing, kernel_ref, ninth_ref):
        heads, ninth = heads_of(ref, base, spacing)
        rest = jnp.dot(ninth_ref[...], ninth, preferred_element_type=jnp.float32)
        return [
            rest[k * channels:(k + 1) * channels]
            + jnp.dot(kernel_ref[...], part, preferred_element_type=jnp.float32)
            for k, part in enumerate(heads)]

    def first(g, _):
        left = left_ref[0, g]
        for j in range(GROUP):
            p = g * GROUP + j
            one = jnp.broadcast_to(left[:, j:j + 1], (channels, TILE))
            pairs = 0.5 * (jnp.concatenate([one] * 3, 0) + right3_ref[...])
            pair_ref[p] = pairs[channels:2 * channels]
            a0_ref[p + DMAX] = jnp.maximum(pairs, 0.0).astype(jnp.bfloat16)
            row = jnp.where(
                sub_c == 0, cot_b[pl.ds(p, 1), :],
                jnp.where(sub_c == 1, cot_f[pl.ds(p, 1), :],
                          jnp.where(sub_c == 2, cot_a[pl.ds(p, 1), :], 0.0)))
            cs_ref[p + DMAX] = row.astype(jnp.bfloat16)
        return 0

    lax.fori_loop(0, TILE // GROUP, first, 0)

    def second_layer(g, _):
        outs = taps_of(a0_ref, g * GROUP, d0, k0_ref, k0n_ref)
        for j in range(0, GROUP, 2):
            p = g * GROUP + j
            out = outs[j // 2]
            for i in range(2):
                value = pair_ref[p + i] + out[:, i * TILE:(i + 1) * TILE]
                pair1_ref[p + i] = value
                put(a1_ref, p + i, jnp.maximum(value, 0.0), d1)
        return 0

    lax.fori_loop(0, TILE // GROUP, second_layer, 0)

    head = head_ref[...]

    def turn(g, carry):
        acc_u, acc_h = carry
        base = g * GROUP
        rows = []
        outs = taps_of(a1_ref, base, d1, k1_ref, k1n_ref)
        cots = jnp.concatenate([
            beside([column(cs_ref, base + DMAX + j + i, d1) for i in range(2)])
            for j in range(0, GROUP, 2)], 0)
        backs = jnp.dot(w1_ref[...], cots, preferred_element_type=jnp.float32)
        for j in range(0, GROUP, 2):
            p = base + j
            out = outs[j // 2]
            back = backs[j // 2 * channels:(j // 2 + 1) * channels]
            for i in range(2):
                value = pair1_ref[p + i]
                cot = cot_f[pl.ds(p + i, 1), :]
                pair2 = value + out[:, i * TILE:(i + 1) * TILE]
                rows.append(jnp.sum(head * pair2, 0, keepdims=True))
                acc_h = acc_h + pair2 * cot
                grad = head * cot + jnp.where(value > 0.0, back[:, i * TILE:(i + 1) * TILE], 0.0)
                pair_ref[p + i] = grad
                put(gs_ref, p + i, grad, d0)
        pred_f[pl.ds(pl.multiple_of(base, GROUP), GROUP), :] = jnp.concatenate(rows, 0)
        every = [base + DMAX + j for j in range(GROUP)]
        acc_u = acc_u + transposed_dot(
            beside([[a1_ref[at]] for at in every]), beside([column(cs_ref, at, d1) for at in every]))
        return acc_u, acc_h

    acc_u, acc_h = lax.fori_loop(
        0, TILE // GROUP, turn, (jnp.zeros(u1_ref.shape, jnp.float32), jnp.zeros(gh_ref.shape, jnp.float32)))
    u1_ref[...] += acc_u
    gh_ref[...] += acc_h
    pred_ref[0] = pred_f[...].astype(jnp.bfloat16)
    mid = slice(channels, 2 * channels)

    def last(g, carry):
        grad_left, grad_right = carry
        base = g * GROUP
        outs = taps_of(gs_ref, base, d0, k0t_ref, k0tn_ref)
        for j in range(0, GROUP, 2):
            p = base + j
            at = p + DMAX
            out = outs[j // 2]
            for i in range(2):
                active = a0_ref[at + i, mid].astype(jnp.float32) > 0.0
                grad = pair_ref[p + i] + jnp.where(active, out[:, i * TILE:(i + 1) * TILE], 0.0)
                grad_right = grad_right + grad
                grad_left = jnp.where(lane == p + i, jnp.sum(grad, 1, keepdims=True), grad_left)
        every = [base + DMAX + j for j in range(GROUP)]
        gk0_ref[...] += transposed_dot(
            beside([[a0_ref[at]] for at in every]),
            beside([[gs_ref[at - d0, mid], gs_ref[at, mid], gs_ref[at + d0, mid]] for at in every]))
        return grad_left, grad_right

    zeros = jnp.zeros((channels, TILE), jnp.float32)
    grad_left, grad_right = lax.fori_loop(0, TILE // GROUP, last, (zeros, zeros))
    gwin_ref[local_row] += 0.5 * grad_left
    gwin_ref[local_row + offset] += 0.5 * grad_right


def tower(tiles, dilation, base_row, window, conv_weight, head_weight, cotangent, total_bins, tile_rows):
    slots = tiles.shape[0]
    channels = window.shape[1]
    blocks = window.shape[0] // TILE
    bf16 = jnp.bfloat16
    f32 = jnp.float32
    window = window.astype(f32)
    left = window[:tile_rows * TILE].reshape(tile_rows, TILE // GROUP, GROUP, channels).transpose(0, 1, 3, 2)
    right = window.reshape(blocks, TILE, channels).transpose(0, 2, 1)
    width = 3 * channels
    taps = 9 * channels
    k0 = conv_weight[0].reshape(taps, channels).T
    k0t = conv_weight[0, ::-1, ::-1].transpose(2, 0, 1, 3).reshape(channels, taps)
    head_f = head_weight.astype(f32)
    folded = jnp.sum(conv_weight[1].astype(f32) * head_f, -1)[::-1, ::-1]
    w1 = jnp.pad(folded, ((0, 0), (0, 13), (0, 0))).transpose(2, 0, 1).reshape(channels, 48).astype(bf16)
    k1 = conv_weight[1].reshape(taps, channels).T
    repeat = jnp.eye(GROUP // 2, dtype=bf16)

    def diagonal(block):
        size = (GROUP // 2 * block.shape[0], GROUP // 2 * block.shape[1])
        return (repeat[:, None, :, None] * block[None, :, None, :]).reshape(size)

    kernels = []
    for kernel in (k0, k1, k0t):
        kernels += [kernel[:, :8 * channels], diagonal(kernel[:, 8 * channels:])]
    kernels += [diagonal(w1), jnp.broadcast_to(head_f[:, None], (channels, TILE))]

    def whole(shape):
        return pl.BlockSpec(shape, lambda s, *_: (0,) * len(shape))

    padded = TILE + 2 * DMAX
    outs = pl.pallas_call(
        partial(tower_kernel, total_bins=total_bins),
        grid_spec=pltpu.PrefetchScalarGridSpec(
            num_scalar_prefetch=3,
            grid=(slots,),
            in_specs=[
                pl.BlockSpec((1, TILE // GROUP, channels, GROUP), lambda s, t, d, b: (t[s] // OFFS, 0, 0, 0)),
                pl.BlockSpec((1, channels, TILE), lambda s, t, d, b: (t[s] // OFFS + t[s] % OFFS, 0, 0)),
                pl.BlockSpec((1, TILE, TILE), lambda s, t, d, b: (s, 0, 0)),
                *[whole(kernel.shape) for kernel in kernels],
            ],
            out_specs=[
                pl.BlockSpec((1, TILE, TILE), lambda s, t, d, b: (s, 0, 0)),
                whole((blocks, channels, TILE)),
                whole((3 * channels, 3 * channels)),
                whole((3 * channels, 48)),
                whole((channels, TILE)),
            ],
            scratch_shapes=[
                pltpu.VMEM((padded, width, TILE), bf16),
                pltpu.VMEM((padded, width, TILE), bf16),
                pltpu.VMEM((padded, width, TILE), bf16),
                pltpu.VMEM((padded, 16, TILE), bf16),
                pltpu.VMEM((TILE, channels, TILE), f32),
                pltpu.VMEM((TILE, channels, TILE), f32),
                pltpu.VMEM((width, TILE), f32),
                pltpu.VMEM((TILE, TILE), f32),
                pltpu.VMEM((TILE, TILE), f32),
                pltpu.VMEM((TILE, TILE), f32),
                pltpu.VMEM((TILE, TILE), f32),
            ],
        ),
        out_shape=[
            jax.ShapeDtypeStruct((slots, TILE, TILE), bf16),
            jax.ShapeDtypeStruct((blocks, channels, TILE), f32),
            jax.ShapeDtypeStruct((3 * channels, 3 * channels), f32),
            jax.ShapeDtypeStruct((3 * channels, 48), f32),
            jax.ShapeDtypeStruct((channels, TILE), f32),
        ],
        compiler_params=pltpu.CompilerParams(
            dimension_semantics=("arbitrary",), vmem_limit_bytes=40 * 1024 * 1024),
        name="tower",
    )(tiles, dilation, base_row, left, right, cotangent, *kernels)
    return outs


def steps_of(size):
    steps, low = [], 1
    while low < size:
        span = min(4, size // low)
        steps.append([low * e for e in range(1, span)])
        low *= span
    return steps


def exchange_kernel(
    rows_n, diag_n, tile_rows, per,
    flat_ref, gwin_ref, sum_ref, bins_ref,
    part_ref, got_ref, near_ref, far_ref, own_got, near_got, far_got,
    sum_send, sum_recv, own_send, own_recv, near_send, near_recv, far_send, far_recv,
):
    g = lax.axis_index("rows")
    d = lax.axis_index("diag")
    count = bins_ref.shape[0]
    mesh_id = pl.DeviceIdType.MESH
    steps = [("rows", e) for e in steps_of(rows_n)] + [("diag", e) for e in steps_of(diag_n)]

    def start_of(index):
        return index * per // TILE

    def at(row, diag):
        return {"rows": row, "diag": diag}

    def partner(axis, e):
        return at(g ^ e, d) if axis == "rows" else at(g, d ^ e)

    barrier = pltpu.get_barrier_semaphore()

    def greet(device):
        pl.semaphore_signal(barrier, inc=1, device_id=device, device_id_type=mesh_id)

    met = 0
    for axis, group in steps:
        for e in group:
            greet(partner(axis, e))
            met += 1
    for e in range(1, diag_n):
        greet(at(g, d ^ e))
        met += 1
    firsts = sum(1 for index in range(diag_n) if index * per // TILE == 0)
    for e in range(diag_n):
        @pl.when(g >= 1)
        def _():
            greet(at(g - 1, d ^ e))

        @pl.when((g >= 2) & (start_of(d) == 0))
        def _():
            greet(at(g - 2, d ^ e))
    to_near = 1 - (g + 1) // rows_n
    to_far = 1 - (g + 2) // rows_n
    pl.semaphore_wait(barrier, met + diag_n * to_near + firsts * to_far)

    def remote(src, dst, send, recv, device):
        return pltpu.make_async_remote_copy(
            src_ref=src, dst_ref=dst, send_sem=send, recv_sem=recv,
            device_id=device, device_id_type=mesh_id)

    def sum_copy(step, slot, axis, e):
        return remote(part_ref.at[step], got_ref.at[slot], sum_send.at[slot], sum_recv.at[slot], partner(axis, e))

    def own_copy(e):
        src = gwin_ref.at[pl.ds(start_of(d ^ e), count)]
        return remote(src, own_got.at[e - 1], own_send.at[e - 1], own_recv.at[e - 1], at(g, d ^ e))

    def near_copy(e):
        src = near_ref.at[pl.ds(start_of(d ^ e), count)]
        return remote(src, near_got.at[e], near_send.at[e], near_recv.at[e], at(g + 1, d ^ e))

    def far_copy(e):
        return remote(far_ref, far_got.at[e], far_send.at[e], far_recv.at[e], at(g + 2, d ^ e))

    sends_near = g + 1 < rows_n
    gets_near = g >= 1
    gets_far = (g >= 2) & (start_of(d) == 0)

    def sends_far(e):
        return (g + 2 < rows_n) & (start_of(d ^ e) == 0)

    near_ref[...] = gwin_ref[tile_rows:2 * tile_rows].astype(jnp.bfloat16)
    far_ref[...] = gwin_ref[2 * tile_rows].astype(jnp.bfloat16)
    slot = 0
    value = flat_ref[...]
    copies = []
    for step, (axis, group) in enumerate(steps):
        part_ref[step] = value.astype(jnp.bfloat16)
        value = part_ref[step].astype(jnp.float32)
        here = [sum_copy(step, slot + i, axis, e) for i, e in enumerate(group)]
        for copy in here:
            copy.start()
        if step == 0:
            for e in range(1, diag_n):
                own_copy(e).start()
            for e in range(diag_n):
                pl.when(sends_near)(near_copy(e).start)
                pl.when(sends_far(e))(far_copy(e).start)
        for copy in here:
            copy.wait_recv()
        others = [got_ref[slot + i].astype(jnp.float32) for i in range(len(group))]
        value = value + others[0]
        if len(group) == 3:
            value = value + (others[1] + others[2])
        slot += len(group)
        copies += here
    sum_ref[...] = value

    bins_ref[...] = gwin_ref[pl.ds(start_of(d), count)]
    for e in range(1, diag_n):
        own_copy(e).wait_recv()
        bins_ref[...] += own_got[e - 1]

    @pl.when(gets_near)
    def _():
        for e in range(diag_n):
            near_copy(e).wait_recv()
            bins_ref[...] += near_got[e].astype(jnp.float32)

    @pl.when(gets_far)
    def _():
        for e in range(diag_n):
            far_copy(e).wait_recv()
            bins_ref[0] += far_got[e].astype(jnp.float32)

    for copy in copies:
        copy.wait_send()
    for e in range(1, diag_n):
        own_copy(e).wait_send()
    for e in range(diag_n):
        pl.when(sends_near)(near_copy(e).wait_send)
        pl.when(sends_far(e))(far_copy(e).wait_send)


def exchange(flat, gwin, tile_rows):
    rows_n = lax.axis_size("rows")
    diag_n = lax.axis_size("diag")
    per = tile_rows * TILE // diag_n
    count = max(1, per // TILE)
    steps = steps_of(rows_n) + steps_of(diag_n)
    slots = sum(len(group) for group in steps)
    channels = gwin.shape[1]
    block = (channels, TILE)
    f32, bf16 = jnp.float32, jnp.bfloat16
    dma = pltpu.SemaphoreType.DMA
    others = max(1, diag_n - 1)
    vmem = pl.BlockSpec(memory_space=pltpu.VMEM)
    total, bins = pl.pallas_call(
        partial(exchange_kernel, rows_n, diag_n, tile_rows, per),
        out_shape=[jax.ShapeDtypeStruct(flat.shape, f32), jax.ShapeDtypeStruct((count,) + block, f32)],
        in_specs=[vmem] * 2,
        out_specs=[vmem] * 2,
        scratch_shapes=[
            pltpu.VMEM((len(steps),) + flat.shape, bf16),
            pltpu.VMEM((slots,) + flat.shape, bf16),
            pltpu.VMEM((tile_rows,) + block, bf16),
            pltpu.VMEM(block, bf16),
            pltpu.VMEM((others, count) + block, f32),
            pltpu.VMEM((diag_n, count) + block, bf16),
            pltpu.VMEM((diag_n,) + block, bf16),
            dma((slots,)), dma((slots,)), dma((others,)), dma((others,)),
            dma((diag_n,)), dma((diag_n,)), dma((diag_n,)), dma((diag_n,)),
        ],
        compiler_params=pltpu.CompilerParams(collective_id=0, has_side_effects=True),
        name="exchange",
    )(flat, gwin)
    bins = bins.transpose(0, 2, 1).reshape(count * TILE, channels)
    if per < TILE:
        inside = lax.axis_index("diag") * per % TILE
        bins = lax.dynamic_slice_in_dim(bins, inside, per, 0)
    return total, bins


def on_device(bins, conv_weight, head_weight, dilation, tile_table, cotangent):
    bin_dev = bins.shape[0]
    channels = bins.shape[1]
    tile_rows = bin_dev // TILE
    total_bins = lax.axis_size("rows") * bin_dev
    following = shifted_2(bins, "rows", -1)
    farther = shifted_2(bins[:TILE], "rows", -2)
    window = jnp.concatenate([bins, following, farther], 0)
    base_row = (lax.axis_index("rows") * tile_rows).astype(jnp.int32).reshape(1)
    predicted, gwin, gk0, u1, gh = tower(
        tile_table[0], dilation, base_row, window, conv_weight, head_weight, cotangent[0],
        total_bins, tile_rows)
    width = 3 * channels
    head_sum = jnp.pad(jnp.sum(gh, 1), (0, width - channels))[:, None]
    flat = jnp.concatenate([gk0, u1[:, 1::16], head_sum], 1)
    flat = jnp.pad(flat, ((0, 0), (0, TILE - flat.shape[1])))
    total, grad_bins = exchange(flat, gwin, tile_rows)
    grad_k0 = total[:, :width].reshape(3, channels, 3, channels)[:, :, ::-1].transpose(2, 0, 1, 3)
    u_sum = total[:, width:width + 3].reshape(3, channels, 3)[:, :, ::-1].transpose(2, 0, 1)
    grad_k1 = u_sum[..., None] * head_weight.astype(jnp.float32)
    grad_head = total[:channels, width + 3]
    return (predicted[None], grad_bins, jnp.stack([grad_k0, grad_k1]), grad_head)


def solution(mesh):
    in_specs = (P("rows", None), P(), P(), P(), P("rows", "diag"), P("rows", "diag", None, None))
    out_specs = (P("rows", "diag", None, None), P(("rows", "diag"), None), P(), P())
    return jax.shard_map(
        on_device, mesh=mesh, in_specs=in_specs, out_specs=out_specs, check_vma=False
    )
```
